256 devices in a mesh: ctx: 16 (over x, y), exp: 16 (over z, core).
Axes of the slice: x: 4, y: 4, z: 8, core: 2. Of those that a mesh axis runs over, the one named last changes fastest.
Arguments:
- queries: bfloat16 [16, 2048, 16, 128], P('exp', 'ctx'), may hold values from -10.5 to 10.5
- keys: bfloat16 [16, 2048, 16, 128], P('exp', 'ctx'), may hold values from -10.5 to 10.5
- values: bfloat16 [16, 2048, 16, 128], P('exp', 'ctx'), may hold values from -6 to 6
- cotangent: bfloat16 [16, 2048, 16, 128], P('exp', 'ctx'), may hold values from -6 to 6
- history: int32 [16, 2048], P('exp', 'ctx'), may hold values from 0 to 1, never falling along the last dimension, each value on 1 to 1536 neighbouring positions
- temper: float32 [16], replicated, may hold values from 0.4 to 1.6
Outputs:
- attn_out: bfloat16 [16, 2048, 16, 128], P('exp', 'ctx')
- grad_queries: bfloat16 [16, 2048, 16, 128], P('exp', 'ctx')
- grad_keys: bfloat16 [16, 2048, 16, 128], P('exp', 'ctx')
- grad_values: bfloat16 [16, 2048, 16, 128], P('exp', 'ctx')
- grad_temper: float32 [16], P('ctx')
The draws below stay inside these ranges and needn't reach their ends.
Inputs may be any that keep to these rules, and one draw needn't show every extreme that they name: Along each batch the history ids never fall; each of the 2 histories holds 1 to 1536 positions.
All inputs are finite; a program needn't handle non-finite values.
Results may differ from the reference program's by a relative error of at most 0.0069.
Values may be sent and summed in bfloat16 or wider, within the bound.
No kernel may reach another device: no remote copies, remote signals or barrier semaphores. Data moves between devices by JAX's collectives and lax.ppermute only.
A program may use at most 64 MiB of HBM per device.

```python
import math
import jax
import jax.numpy as jnp
import numpy as np
from jax import lax

HEADS = 16
HD = 128
HISTS = 2
SEQ = 2048
BATCHES = 16


def shared_law(key):
    temper = jnp.exp(jax.random.uniform(jax.random.fold_in(key, 101), (HEADS,), jnp.float32, jnp.log(0.4), jnp.log(1.6)))
    paired = jax.random.bernoulli(jax.random.fold_in(key, 102), 1.0 / 16, (BATCHES, SEQ // 2))
    levels = jax.random.randint(jax.random.fold_in(key, 103), (BATCHES, SEQ // 2), 1, 4).astype(jnp.float32) * 60.0 + 50.0
    sign_vectors = jax.random.rademacher(jax.random.fold_in(key, 104), (BATCHES, SEQ // 2, HEADS, HD), jnp.float32)
    amplitude = jnp.sqrt(levels[:, :, None, None] / (temper[None, None, :, None] * HD ** 0.5))
    return (temper, paired, levels, amplitude * sign_vectors)


def draw_temper(key, part):
    common = shared_law(key)
    return common[0]


def draw_queries(key, part):
    key = jax.random.fold_in(key, 7)
    background = jax.random.truncated_normal(key, -4.0, 4.0, (BATCHES, SEQ, HEADS, HD), jnp.float32)
    return background.astype(jnp.bfloat16)


def draw_keys(key, part):
    key = jax.random.fold_in(key, 9)
    background = jax.random.truncated_normal(key, -4.0, 4.0, (BATCHES, SEQ, HEADS, HD), jnp.float32)
    return background.astype(jnp.bfloat16)


def level_of(own_key, dims, split, low, high):
    def one(position, parts):
        steps = jax.random.uniform(jax.random.fold_in(jax.random.fold_in(own_key, 6), position), (parts,), jnp.float32, low / len(split), high / len(split))
        return jnp.repeat(jnp.exp(steps), dims[position] // parts).reshape((-1,) + (1,) * (len(dims) - position - 1))

    gain = one(*split[0])
    for cut in split[1:]:
        gain = gain * one(*cut)
    return gain


def profile(count, total, reach, skew):
    loads = [(1 << 20) // math.isqrt(standing ** skew) + 1 for standing in range(2, count + 1)]
    surplus, counts = total - reach - (count - 1), [1] * (count - 1)
    while surplus > 0:
        free = [i for i in range(count - 1) if counts[i] < reach]
        pool, left = sum([loads[i] for i in free]), surplus
        for i in free:
            extra = min(reach - counts[i], max(1, left * loads[i] // pool), surplus)
            counts[i] = counts[i] + extra
            surplus = surplus - extra
    return np.array([reach] + counts)


def ragged(own_key, amount, total, most, slope):
    if amount == 2:
        one = jax.random.randint(own_key, (), max(1, total - most), min(most, total - 1) + 1)
        return jnp.stack([one, total - one])
    sizes = jnp.asarray(profile(amount, total, most, slope), jnp.int32)
    couples = (amount - 1) // 2
    source_of, taker = sizes[1:1 + 2 * couples:2], sizes[2:2 + 2 * couples:2]
    slack = jnp.minimum(source_of - 1, most - taker)
    passed = jax.random.randint(jax.random.fold_in(own_key, 1), (couples,), 0, 1 << 20) % (slack + 1)
    sizes = sizes.at[1:1 + 2 * couples:2].set(source_of - passed).at[2:2 + 2 * couples:2].set(taker + passed)
    return sizes[jax.random.permutation(jax.random.fold_in(own_key, 2), amount)]


def centred(stream_key, shape, width, bound, split=(), kind=jnp.bfloat16):
    array = width * jax.random.normal(stream_key, shape, jnp.float32)
    if split:
        array = array * level_of(stream_key, shape, split, -0.22, 0.18)
    return jnp.clip(array, -bound, bound).astype(kind)


def setup_inputs(seed: int = 0) -> dict:
    seeds = jax.random.split(jax.random.key(seed), 7)
    return {
        "queries": draw_queries(jax.random.fold_in(seeds[6], 71), 0),
        "keys": draw_keys(jax.random.fold_in(seeds[6], 71), 0),
        "values": centred(seeds[2], (BATCHES, SEQ, HEADS, HD), 1.0, 6.0, ((0, 16), (1, 16))),
        "cotangent": centred(seeds[3], (BATCHES, SEQ, HEADS, HD), 1.0, 6.0, ((0, 16), (1, 16))),
        "history": jax.vmap(lambda own: jnp.searchsorted(jnp.cumsum(ragged(own, HISTS, SEQ, SEQ * 3 // 4, 2)), jnp.arange(SEQ), side="right"))(jax.random.split(seeds[4], BATCHES)).reshape((BATCHES, SEQ)).astype(jnp.int32),
        "temper": draw_temper(jax.random.fold_in(seeds[6], 71), 0),
    }


def one_head(head_queries, head_keys, head_values, head_cotangent, history_ids, head_temper):
    inv_root = HD ** -0.5
    raw_scores = jnp.dot(head_queries, head_keys.T, preferred_element_type=jnp.float32) * inv_root
    positions = jnp.arange(SEQ, dtype=jnp.int32)
    allowed = (history_ids[:, None] == history_ids[None, :]) & (positions[:, None] >= positions[None, :])
    logits = jnp.where(allowed, raw_scores * head_temper, -jnp.inf)
    row_max = jnp.max(logits, axis=-1, keepdims=True)
    exponents = jnp.exp(logits - row_max)
    probabilities = exponents / jnp.sum(exponents, axis=-1, keepdims=True)
    weights = probabilities.astype(jnp.bfloat16)
    attn_out = jnp.dot(weights, head_values, preferred_element_type=jnp.float32).astype(jnp.bfloat16)
    prob_grads = jnp.dot(head_cotangent, head_values.T, preferred_element_type=jnp.float32)
    row_delta = jnp.sum(probabilities * prob_grads, axis=-1, keepdims=True)
    score_grads = probabilities * (prob_grads - row_delta)
    score_low = (score_grads * (head_temper * inv_root)).astype(jnp.bfloat16)
    grad_queries = jnp.dot(score_low, head_keys, preferred_element_type=jnp.float32).astype(jnp.bfloat16)
    grad_keys = jnp.dot(score_low.T, head_queries, preferred_element_type=jnp.float32).astype(jnp.bfloat16)
    grad_values = jnp.dot(weights.T, head_cotangent, preferred_element_type=jnp.float32).astype(jnp.bfloat16)
    grad_temper = jnp.sum(score_grads * raw_scores)
    return attn_out, grad_queries, grad_keys, grad_values, grad_temper


def reference(queries, keys, values, cotangent, history, temper):
    def one_batch(batch_inputs):
        batch_q, batch_k, batch_v, batch_c, history_ids = batch_inputs

        def per_head(head_inputs):
            head_q, head_k, head_v, head_c, head_t = head_inputs
            return one_head(head_q, head_k, head_v, head_c, history_ids, head_t)

        return lax.map(per_head, (jnp.moveaxis(batch_q, 1, 0), jnp.moveaxis(batch_k, 1, 0), jnp.moveaxis(batch_v, 1, 0), jnp.moveaxis(batch_c, 1, 0), temper))

    results = lax.map(one_batch, (queries, keys, values, cotangent, history))
    attn_out = jnp.moveaxis(results[0], 1, 2)
    grad_queries = jnp.moveaxis(results[1], 1, 2)
    grad_keys = jnp.moveaxis(results[2], 1, 2)
    grad_values = jnp.moveaxis(results[3], 1, 2)
    grad_temper = jnp.sum(results[4], axis=0)
    return (attn_out, grad_queries, grad_keys, grad_values, grad_temper)
```

```python
import functools

import jax
import jax.numpy as jnp
from jax import lax
from jax.experimental import pallas as pl
from jax.experimental.pallas import tpu as pltpu
from jax.sharding import PartitionSpec as P

NT = (((1,), (1,)), ((), ()))
NN = (((1,), (0,)), ((), ()))
LOG2E = 1.4426950408889634
HIDE = -1e30
BLK = 256
PAD = 16
VMEM_LIMIT = 56 * 1024 * 1024


def dot(a, b, dims):
    return lax.dot_general(a, b, dims, preferred_element_type=jnp.float32)


def pack_body(q_ref, k_ref, v_ref, c_ref, hist_ref, out_ref, wide):
    rows, heads, hd = q_ref.shape
    for place, ref in enumerate((q_ref, k_ref, v_ref, c_ref)):
        wide[place] = ref[...].astype(jnp.float32).reshape(rows * heads, hd)
        for head in range(heads):
            part = wide[place, pl.ds(head, rows, stride=heads), :]
            out_ref[head, place * rows : (place + 1) * rows, :] = part.astype(jnp.bfloat16)
    ids = jnp.broadcast_to(hist_ref[...].astype(jnp.float32), (PAD, rows)).astype(jnp.bfloat16)
    for head in range(heads):
        out_ref[head, 4 * rows :, :] = ids


def unpack_body(in_ref, a_ref, b_ref, c_ref, d_ref, wide):
    rows, heads, hd = a_ref.shape
    for place, ref in enumerate((a_ref, b_ref, c_ref, d_ref)):
        for head in range(heads):
            part = in_ref[head, place * rows : (place + 1) * rows, :]
            wide[place, pl.ds(head, rows, stride=heads), :] = part.astype(jnp.float32)
        ref[...] = wide[place].reshape(rows, heads, hd).astype(jnp.bfloat16)


def attend_body(
    temper_ref, in_ref, out_ref, gt_ref, logit, pgrad, k_t, v_t, dk_acc, dv_acc, o_acc, dq_acc
):
    shards, _, hd = in_ref.shape
    rows = 128
    per = BLK // rows
    blocks = shards // per
    seq = shards * rows
    temper = temper_ref[lax.axis_index("ctx")]
    inv_root = hd ** (-0.5)
    logit_scale = temper * (inv_root * LOG2E)

    ids = in_ref[:, 4 * rows :, :].astype(jnp.float32)
    later = jnp.sum(ids) * (1.0 / PAD)
    bound = seq - later.astype(jnp.int32)

    def rows_of(place, block):
        part = in_ref[pl.ds(block * per, per), place * rows : (place + 1) * rows, :]
        return part.reshape(BLK, hd)

    def identity(size):
        return (
            lax.broadcasted_iota(jnp.int32, (size, size), 0)
            == lax.broadcasted_iota(jnp.int32, (size, size), 1)
        ).astype(jnp.bfloat16)

    eye_hd = identity(hd)
    eye_blk = identity(BLK)

    def prepare(block, carry):
        k_t[block] = dot(eye_hd, rows_of(1, block), NT).astype(jnp.bfloat16)
        v_t[block] = dot(eye_hd, rows_of(2, block), NT).astype(jnp.bfloat16)
        dk_acc[block] = jnp.zeros((BLK, hd), jnp.float32)
        dv_acc[block] = jnp.zeros((BLK, hd), jnp.float32)
        return carry

    lax.fori_loop(0, blocks, prepare, 0)

    def query_block(i, gt):
        q_i = rows_of(0, i)
        c_i = rows_of(3, i)
        first_i = i * BLK
        start = jnp.where(first_i >= bound, bound // BLK, 0)
        i_splits = (first_i < bound) & (bound < first_i + BLK)

        def scan_keys(j, carry):
            top, total, delta = carry
            first_j = j * BLK
            s = dot(rows_of(1, j), q_i, NT) * logit_scale
            hides = (j == i) | i_splits | ((first_j < bound) & (bound < first_j + BLK))

            def hide(s):
                row = first_j + lax.broadcasted_iota(jnp.int32, (BLK, BLK), 0)
                col = first_i + lax.broadcasted_iota(jnp.int32, (BLK, BLK), 1)
                low = jnp.where(col >= bound, bound, 0)
                return jnp.where((row <= col) & (row >= low), s, HIDE)

            logit[j] = s

            @pl.when(hides)
            def _():
                logit[j] = hide(s)

            s = logit[j].reshape(BLK // 8, 8, BLK)
            g = dot(rows_of(2, j), c_i, NT)
            pgrad[j] = g
            new_top = jnp.maximum(top, jnp.max(s, axis=0))
            keep = jnp.exp2(top - new_top)
            e = jnp.exp2(s - new_top[None])
            total = total * keep + jnp.sum(e, axis=0)
            delta = delta * keep + jnp.sum(e * g.reshape(BLK // 8, 8, BLK), axis=0)
            return new_top, total, delta

        zero = jnp.zeros((8, BLK), jnp.float32)
        top, total, delta = lax.fori_loop(
            start, i + 1, scan_keys, (jnp.full((8, BLK), HIDE, jnp.float32), zero, zero)
        )
        top_all = jnp.max(top, axis=0, keepdims=True)
        part = jnp.exp2(top - top_all)
        total = jnp.sum(total * part, axis=0, keepdims=True)
        delta = jnp.sum(delta * part, axis=0, keepdims=True) / total
        norm = top_all + jnp.log2(total)
        o_acc[...] = jnp.zeros((hd, BLK), jnp.float32)
        dq_acc[...] = jnp.zeros((hd, BLK), jnp.float32)

        def gradients(j, gt):
            s = logit[j]
            p = jnp.exp2(s - norm)
            ds = p * (pgrad[j] - delta)
            gt = gt + jnp.sum((ds * s).reshape(BLK // 8, 8, BLK), axis=0)
            p_low = p.astype(jnp.bfloat16)
            ds_low = ds.astype(jnp.bfloat16)
            dv_acc[j] += dot(p_low, c_i, NN)
            dk_acc[j] += dot(ds_low, q_i, NN)
            o_acc[...] += dot(v_t[j], p_low, NN)
            dq_acc[...] += dot(k_t[j], ds_low, NN)
            return gt

        gt = lax.fori_loop(start, i + 1, gradients, gt)
        o = dot(eye_blk, o_acc[...].astype(jnp.bfloat16), NT).astype(jnp.bfloat16)
        dq = (dq_acc[...] * (temper * inv_root)).astype(jnp.bfloat16)
        dq = dot(eye_blk, dq, NT).astype(jnp.bfloat16)
        out_ref[pl.ds(i * per, per), 0:rows, :] = o.reshape(per, rows, hd)
        out_ref[pl.ds(i * per, per), rows : 2 * rows, :] = dq.reshape(per, rows, hd)
        return gt

    gt = lax.fori_loop(0, blocks, query_block, jnp.zeros((8, BLK), jnp.float32))

    def finish(block, carry):
        dk = (dk_acc[block] * (temper * inv_root)).astype(jnp.bfloat16)
        dv = dv_acc[block].astype(jnp.bfloat16)
        out_ref[pl.ds(block * per, per), 2 * rows : 3 * rows, :] = dk.reshape(per, rows, hd)
        out_ref[pl.ds(block * per, per), 3 * rows : 4 * rows, :] = dv.reshape(per, rows, hd)
        return carry

    lax.fori_loop(0, blocks, finish, 0)
    gt_ref[0] = jnp.sum(gt) / (temper * LOG2E)


def vmem_spec():
    return pl.BlockSpec(memory_space=pltpu.VMEM)


def body(queries, keys, values, cotangent, history, temper):
    _, rows, heads, hd = queries.shape
    shards = lax.axis_size("ctx")
    blocks = shards * rows // BLK
    params = pltpu.CompilerParams(vmem_limit_bytes=VMEM_LIMIT)
    low, f32 = jnp.bfloat16, jnp.float32

    send = pl.pallas_call(
        pack_body,
        out_shape=jax.ShapeDtypeStruct((heads, 4 * rows + PAD, hd), low),
        in_specs=[vmem_spec()] * 5,
        out_specs=vmem_spec(),
        scratch_shapes=[pltpu.VMEM((4, rows * heads, hd), f32)],
        compiler_params=params,
    )(queries[0], keys[0], values[0], cotangent[0], history)
    recv = lax.all_to_all(send, "ctx", split_axis=0, concat_axis=0, tiled=True)
    results, gt = pl.pallas_call(
        attend_body,
        out_shape=(
            jax.ShapeDtypeStruct((shards, 4 * rows, hd), low),
            jax.ShapeDtypeStruct((1,), f32),
        ),
        in_specs=[pl.BlockSpec(memory_space=pltpu.SMEM), vmem_spec()],
        out_specs=(vmem_spec(), pl.BlockSpec(memory_space=pltpu.SMEM)),
        scratch_shapes=[
            pltpu.VMEM((blocks, BLK, BLK), f32),
            pltpu.VMEM((blocks, BLK, BLK), f32),
            pltpu.VMEM((blocks, hd, BLK), low),
            pltpu.VMEM((blocks, hd, BLK), low),
            pltpu.VMEM((blocks, BLK, hd), f32),
            pltpu.VMEM((blocks, BLK, hd), f32),
            pltpu.VMEM((hd, BLK), f32),
            pltpu.VMEM((hd, BLK), f32),
        ],
        compiler_params=params,
    )(temper, recv)
    back = lax.all_to_all(results, "ctx", split_axis=0, concat_axis=0, tiled=True)
    exp_size = lax.axis_size("exp")
    step = 1
    while step < exp_size:
        gt = gt + lax.ppermute(gt, "exp", [(n, (n + step) % exp_size) for n in range(exp_size)])
        step *= 2
    outs = pl.pallas_call(
        unpack_body,
        out_shape=[jax.ShapeDtypeStruct((rows, heads, hd), low)] * 4,
        in_specs=[vmem_spec()],
        out_specs=[vmem_spec()] * 4,
        scratch_shapes=[pltpu.VMEM((4, rows * heads, hd), f32)],
        compiler_params=params,
    )(back)
    attn_out, grad_q, grad_k, grad_v = [part[None] for part in outs]
    return attn_out, grad_q, grad_k, grad_v, gt


def solution(mesh):
    placed = P("exp", "ctx", None, None)
    return jax.shard_map(
        body,
        mesh=mesh,
        in_specs=(placed, placed, placed, placed, P("exp", "ctx"), P()),
        out_specs=(placed, placed, placed, placed, P("ctx")),
        check_vma=False,
    )
```

```python
import math

import jax
import jax.numpy as jnp
from jax import lax
from jax.experimental import pallas as pl
from jax.experimental.pallas import tpu as pltpu
from jax.sharding import PartitionSpec as P

NT = (((1,), (1,)), ((), ()))
NN = (((1,), (0,)), ((), ()))
LOG2E = 1.4426950408889634
HIDE = -1e30
BLK = 512
PAD = 16
MIB = 1024 * 1024


def offsets(size):
    side = math.isqrt(size)
    steps = [(dx, dy) for dx in range(side) for dy in range(side) if (dx, dy) != (0, 0)]
    return side, sorted(steps, key=lambda s: -sum(min(d, side - d) for d in s))


def moved(index, step, side):
    return (index // side + step[0]) % side * side + (index % side + step[1]) % side


def exchange(parts, axis):
    size = len(parts)
    side, steps = offsets(size)
    got = [parts[0]]
    for part, step in zip(parts[1:], steps):
        got.append(lax.ppermute(part, axis, [(n, moved(n, step, side)) for n in range(size)]))
    return got


def targets(me, size, sign):
    side, steps = offsets(size)
    ends = [me]
    for dx, dy in steps:
        x = lax.rem(lax.div(me, side) + side + sign * dx, side)
        y = lax.rem(lax.rem(me, side) + side + sign * dy, side)
        ends.append(x * side + y)
    return ends


def dot(a, b, dims):
    return lax.dot_general(a, b, dims, preferred_element_type=jnp.float32)


def pack_body(q_hbm, k_hbm, v_hbm, c_hbm, hist_ref, *refs):
    *outs, held, wide, packed, in_sem, out_sem = refs
    _, rows, heads, hd = held.shape
    ends = targets(lax.axis_index("ctx"), heads, 1)
    loads = [
        pltpu.make_async_copy(ref, held.at[place], in_sem.at[place])
        for place, ref in enumerate((q_hbm, k_hbm, v_hbm, c_hbm))
    ]
    for load in loads:
        load.start()
    ids = jnp.broadcast_to(hist_ref[...].astype(jnp.float32), (PAD, rows)).astype(jnp.bfloat16)
    for head in range(heads):
        packed[head, 4 * rows :, :] = ids
    stores = []
    for place, load in enumerate(loads):
        load.wait()
        wide[place % 2] = held[place].astype(jnp.float32).reshape(rows * heads, hd)
        for head in range(heads):
            part = wide[place % 2, pl.ds(head, rows, stride=heads), :]
            packed[head, place * rows : (place + 1) * rows, :] = part.astype(jnp.bfloat16)
        if place % 2 == 0:
            continue
        span = pl.ds((place - 1) * rows, 2 * rows if place < 3 else 2 * rows + PAD)
        for n, (out, end) in enumerate(zip(outs, ends)):
            store = pltpu.make_async_copy(
                packed.at[end, span, :], out.at[span, :], out_sem.at[place // 2, n]
            )
            store.start()
            stores.append(store)
    for store in stores:
        store.wait()


def unpack_body(*refs):
    held, wide, packed, in_sem, out_sem = refs[-5:]
    _, rows, heads, hd = packed.shape
    ins, outs = refs[:heads], refs[heads:-5]
    ends = targets(lax.axis_index("ctx"), heads, -1)
    loads = [[] for _ in range(4)]
    for place in range(4):
        span = pl.ds(place * rows, rows)
        for n, (ref, end) in enumerate(zip(ins, ends)):
            load = pltpu.make_async_copy(
                ref.at[span, :], held.at[end, span, :], in_sem.at[place, n]
            )
            load.start()
            loads[place].append(load)
    stores = []
    for place, ref in enumerate(outs):
        for load in loads[place]:
            load.wait()
        for head in range(heads):
            part = held[head, place * rows : (place + 1) * rows, :]
            wide[place % 2, pl.ds(head, rows, stride=heads), :] = part.astype(jnp.float32)
        packed[place] = wide[place % 2].reshape(rows, heads, hd).astype(jnp.bfloat16)
        store = pltpu.make_async_copy(packed.at[place], ref, out_sem.at[place])
        store.start()
        stores.append(store)
    for store in stores:
        store.wait()


def attend_body(temper_ref, *refs):
    in_ref, out_ref, logit, pgrad, k_t, v_t, dk_acc, dv_acc, o_acc, dq_acc, sem = refs[-11:]
    shards, _, hd = in_ref.shape
    ins, outs, gt_ref = refs[:shards], refs[shards : 2 * shards], refs[2 * shards]
    me = lax.axis_index("ctx")
    loads = []
    for n, (ref, end) in enumerate(zip(ins, targets(me, shards, -1))):
        load = pltpu.make_async_copy(ref, in_ref.at[end], sem.at[n])
        load.start()
        loads.append(load)
    for load in loads:
        load.wait()
    rows = 128
    per = BLK // rows
    blocks = shards // per
    seq = shards * rows
    temper = temper_ref[me]
    inv_root = hd ** (-0.5)
    logit_scale = temper * (inv_root * LOG2E)

    ids = in_ref[:, 4 * rows :, :].astype(jnp.float32)
    later = jnp.sum(ids) * (1.0 / PAD)
    bound = seq - later.astype(jnp.int32)

    def rows_of(place, block):
        part = in_ref[pl.ds(block * per, per), place * rows : (place + 1) * rows, :]
        return part.reshape(BLK, hd)

    def identity(size):
        return (
            lax.broadcasted_iota(jnp.int32, (size, size), 0)
            == lax.broadcasted_iota(jnp.int32, (size, size), 1)
        ).astype(jnp.bfloat16)

    eye_hd = identity(hd)
    eye_blk = identity(BLK)

    def prepare(block, carry):
        k_t[block] = dot(eye_hd, rows_of(1, block), NT).astype(jnp.bfloat16)
        v_t[block] = dot(eye_hd, rows_of(2, block), NT).astype(jnp.bfloat16)
        dk_acc[block] = jnp.zeros((BLK, hd), jnp.float32)
        dv_acc[block] = jnp.zeros((BLK, hd), jnp.float32)
        return carry

    lax.fori_loop(0, blocks, prepare, 0, unroll=True)

    def query_block(i, gt):
        q_i = rows_of(0, i)
        c_i = rows_of(3, i)
        first_i = i * BLK
        start = jnp.where(first_i >= bound, bound // BLK, 0)
        cols = first_i + lax.broadcasted_iota(jnp.int32, (1, BLK), 1)
        low = jnp.where(cols >= bound, bound, 0)

        def scan_keys(j, carry):
            top, total, delta = carry
            first_j = j * BLK
            s = dot(rows_of(1, j), q_i, NT) * logit_scale
            row = first_j + lax.broadcasted_iota(jnp.int32, (BLK, BLK), 0)
            col = first_i + lax.broadcasted_iota(jnp.int32, (BLK, BLK), 1)
            s = jnp.where((row <= col) & (row >= low), s, HIDE)
            logit[j] = s
            s = s.reshape(BLK // 8, 8, BLK)
            g = dot(rows_of(2, j), c_i, NT)
            pgrad[j] = g
            new_top = jnp.maximum(top, jnp.max(s, axis=0))
            keep = jnp.exp2(top - new_top)
            e = jnp.exp2(s - new_top[None])
            total = total * keep + jnp.sum(e, axis=0)
            delta = delta * keep + jnp.sum(e * g.reshape(BLK // 8, 8, BLK), axis=0)
            return new_top, total, delta

        zero = jnp.zeros((8, BLK), jnp.float32)
        top, total, delta = lax.fori_loop(
            start, i + 1, scan_keys, (jnp.full((8, BLK), HIDE, jnp.float32), zero, zero)
        )
        top_all = jnp.max(top, axis=0, keepdims=True)
        part = jnp.exp2(top - top_all)
        total = jnp.sum(total * part, axis=0, keepdims=True)
        delta = jnp.sum(delta * part, axis=0, keepdims=True) / total
        norm = top_all + jnp.log2(total)
        o_acc[...] = jnp.zeros((hd, BLK), jnp.float32)
        dq_acc[...] = jnp.zeros((hd, BLK), jnp.float32)

        def gradients(j, gt):
            s = logit[j]
            p = jnp.exp2(s - norm)
            ds = p * (pgrad[j] - delta)
            gt = gt + jnp.sum((ds * s).reshape(BLK // 8, 8, BLK), axis=0)
            p_low = p.astype(jnp.bfloat16)
            ds_low = ds.astype(jnp.bfloat16)
            dv_acc[j] += dot(p_low, c_i, NN)
            dk_acc[j] += dot(ds_low, q_i, NN)
            o_acc[...] += dot(v_t[j], p_low, NN)
            dq_acc[...] += dot(k_t[j], ds_low, NN)
            return gt

        gt = lax.fori_loop(start, i + 1, gradients, gt)
        o = dot(eye_blk, o_acc[...].astype(jnp.bfloat16), NT).astype(jnp.bfloat16)
        dq = (dq_acc[...] * (temper * inv_root)).astype(jnp.bfloat16)
        dq = dot(eye_blk, dq, NT).astype(jnp.bfloat16)
        out_ref[pl.ds(i * per, per), 0:rows, :] = o.reshape(per, rows, hd)
        out_ref[pl.ds(i * per, per), rows : 2 * rows, :] = dq.reshape(per, rows, hd)
        return gt

    gt = lax.fori_loop(0, blocks, query_block, jnp.zeros((8, BLK), jnp.float32))

    def finish(block, carry):
        dk = (dk_acc[block] * (temper * inv_root)).astype(jnp.bfloat16)
        dv = dv_acc[block].astype(jnp.bfloat16)
        out_ref[pl.ds(block * per, per), 2 * rows : 3 * rows, :] = dk.reshape(per, rows, hd)
        out_ref[pl.ds(block * per, per), 3 * rows : 4 * rows, :] = dv.reshape(per, rows, hd)
        return carry

    lax.fori_loop(0, blocks, finish, 0, unroll=True)
    gt_ref[0] = jnp.sum(gt) / (temper * LOG2E)
    stores = []
    for n, (ref, end) in enumerate(zip(outs, targets(me, shards, 1))):
        store = pltpu.make_async_copy(out_ref.at[end], ref, sem.at[n])
        store.start()
        stores.append(store)
    for store in stores:
        store.wait()


def vmem_spec():
    return pl.BlockSpec(memory_space=pltpu.VMEM)


def any_spec():
    return pl.BlockSpec(memory_space=pl.ANY)


def grant(mib):
    return pltpu.CompilerParams(vmem_limit_bytes=mib * MIB)


def body(queries, keys, values, cotangent, history, temper):
    _, rows, heads, hd = queries.shape
    shards = lax.axis_size("ctx")
    blocks = shards * rows // BLK
    low, f32 = jnp.bfloat16, jnp.float32

    sends = pl.pallas_call(
        pack_body,
        out_shape=[jax.ShapeDtypeStruct((4 * rows + PAD, hd), low)] * heads,
        in_specs=[any_spec()] * 4 + [vmem_spec()],
        out_specs=[any_spec()] * heads,
        scratch_shapes=[
            pltpu.VMEM((4, rows, heads, hd), low),
            pltpu.VMEM((2, rows * heads, hd), f32),
            pltpu.VMEM((heads, 4 * rows + PAD, hd), low),
            pltpu.SemaphoreType.DMA((4,)),
            pltpu.SemaphoreType.DMA((2, heads)),
        ],
        compiler_params=grant(56),
    )(queries[0], keys[0], values[0], cotangent[0], history)
    received = exchange(sends, "ctx")
    smem_spec = pl.BlockSpec(memory_space=pltpu.SMEM)
    *results, gt = pl.pallas_call(
        attend_body,
        out_shape=[jax.ShapeDtypeStruct((4 * rows, hd), low)] * shards
        + [jax.ShapeDtypeStruct((1,), f32)],
        in_specs=[smem_spec] + [any_spec()] * shards,
        out_specs=[any_spec()] * shards + [smem_spec],
        scratch_shapes=[
            pltpu.VMEM((shards, 4 * rows + PAD, hd), low),
            pltpu.VMEM((shards, 4 * rows, hd), low),
            pltpu.VMEM((blocks, BLK, BLK), f32),
            pltpu.VMEM((blocks, BLK, BLK), f32),
            pltpu.VMEM((blocks, hd, BLK), low),
            pltpu.VMEM((blocks, hd, BLK), low),
            pltpu.VMEM((blocks, BLK, hd), f32),
            pltpu.VMEM((blocks, BLK, hd), f32),
            pltpu.VMEM((hd, BLK), f32),
            pltpu.VMEM((hd, BLK), f32),
            pltpu.SemaphoreType.DMA((shards,)),
        ],
        compiler_params=grant(56),
    )(temper, *received)
    back = exchange(results, "ctx")
    exp_size = lax.axis_size("exp")
    step = 1
    while step < exp_size:
        gt = gt + lax.ppermute(gt, "exp", [(n, (n + step) % exp_size) for n in range(exp_size)])
        step *= 2
    outs = pl.pallas_call(
        unpack_body,
        out_shape=[jax.ShapeDtypeStruct((rows, heads, hd), low)] * 4,
        in_specs=[any_spec()] * shards,
        out_specs=[any_spec()] * 4,
        scratch_shapes=[
            pltpu.VMEM((heads, 4 * rows, hd), low),
            pltpu.VMEM((2, rows * heads, hd), f32),
            pltpu.VMEM((4, rows, heads, hd), low),
            pltpu.SemaphoreType.DMA((4, shards)),
            pltpu.SemaphoreType.DMA((4,)),
        ],
        compiler_params=grant(24),
    )(*back)
    attn_out, grad_q, grad_k, grad_v = [part[None] for part in outs]
    return attn_out, grad_q, grad_k, grad_v, gt


def solution(mesh):
    placed = P("exp", "ctx", None, None)
    return jax.shard_map(
        body,
        mesh=mesh,
        in_specs=(placed, placed, placed, placed, P("exp", "ctx"), P()),
        out_specs=(placed, placed, placed, placed, P("ctx")),
        check_vma=False,
    )
```

```python
import functools

import jax
import jax.numpy as jnp
from jax import lax
from jax.experimental import pallas as pl
from jax.experimental.pallas import tpu as pltpu
from jax.sharding import PartitionSpec as P

NT = (((1,), (1,)), ((), ()))
NN = (((1,), (0,)), ((), ()))
LOG2E = 1.4426950408889634
HIDE = -1e30
BLK = 256
PAD = 16
MIB = 1024 * 1024


def dot(a, b, dims):
    return lax.dot_general(a, b, dims, preferred_element_type=jnp.float32)


def pack_body(q_hbm, k_hbm, v_hbm, c_hbm, hist_ref, out_hbm, held, wide, packed, in_sem, out_sem):
    _, rows, heads, hd = held.shape
    loads = [
        pltpu.make_async_copy(ref, held.at[place], in_sem.at[place])
        for place, ref in enumerate((q_hbm, k_hbm, v_hbm, c_hbm))
    ]
    for load in loads:
        load.start()
    ids = jnp.broadcast_to(hist_ref[...].astype(jnp.float32), (PAD, rows)).astype(jnp.bfloat16)
    for head in range(heads):
        packed[head, 4 * rows :, :] = ids
    stores = []
    for place, load in enumerate(loads):
        load.wait()
        wide[place % 2] = held[place].astype(jnp.float32).reshape(rows * heads, hd)
        for head in range(heads):
            part = wide[place % 2, pl.ds(head, rows, stride=heads), :]
            packed[head, place * rows : (place + 1) * rows, :] = part.astype(jnp.bfloat16)
        span = pl.ds(place * rows, rows if place < 3 else rows + PAD)
        store = pltpu.make_async_copy(
            packed.at[:, span, :], out_hbm.at[:, span, :], out_sem.at[place]
        )
        store.start()
        stores.append(store)
    for store in stores:
        store.wait()


def unpack_body(in_hbm, a_hbm, b_hbm, c_hbm, d_hbm, held, wide, packed, in_sem, out_sem):
    _, rows, heads, hd = packed.shape
    loads = []
    for place in range(4):
        span = pl.ds(place * rows, rows)
        load = pltpu.make_async_copy(
            in_hbm.at[:, span, :], held.at[:, span, :], in_sem.at[place]
        )
        load.start()
        loads.append(load)
    stores = []
    for place, ref in enumerate((a_hbm, b_hbm, c_hbm, d_hbm)):
        loads[place].wait()
        for head in range(heads):
            part = held[head, place * rows : (place + 1) * rows, :]
            wide[place % 2, pl.ds(head, rows, stride=heads), :] = part.astype(jnp.float32)
        packed[place] = wide[place % 2].reshape(rows, heads, hd).astype(jnp.bfloat16)
        store = pltpu.make_async_copy(packed.at[place], ref, out_sem.at[place])
        store.start()
        stores.append(store)
    for store in stores:
        store.wait()


def attend_body(
    temper_ref,
    in_hbm,
    out_hbm,
    gt_ref,
    held,
    done,
    logit,
    pgrad,
    k_t,
    v_t,
    dk_acc,
    dv_acc,
    in_sem,
    out_sem,
):
    shards, hd = held.shape[0], held.shape[2]
    rows = done.shape[1] // 4
    per = BLK // rows
    blocks = shards // per
    group = blocks // 4
    loads = [
        pltpu.make_async_copy(in_hbm.at[span], held.at[span], in_sem.at[n])
        for n, span in enumerate(
            (pl.ds(0, group * per), pl.ds(group * per, shards - group * per))
        )
    ]
    for load in loads:
        load.start()
    temper = temper_ref[lax.axis_index("ctx")]
    scale = temper * hd ** (-0.5)
    logit_scale = scale * LOG2E

    def identity(size):
        return (
            lax.broadcasted_iota(jnp.int32, (size, size), 0)
            == lax.broadcasted_iota(jnp.int32, (size, size), 1)
        ).astype(jnp.bfloat16)

    eye_hd = identity(hd)
    eye_blk = identity(BLK)

    def span_of(place, low, high):
        part = held[low * per : high * per, place * rows : (place + 1) * rows, :]
        return part.reshape((high - low) * BLK, hd)

    def put(place, block, value):
        done[block * per : (block + 1) * per, place * rows : (place + 1) * rows, :] = value.astype(
            jnp.bfloat16
        ).reshape(per, rows, hd)

    def store(first, last, kind):
        span, part = pl.ds(first * per, (last - first) * per), pl.ds(2 * kind * rows, 2 * rows)
        return pltpu.make_async_copy(
            done.at[span, part, :], out_hbm.at[span, part, :], out_sem.at[kind, first // group]
        )

    def turn(low, high):
        span = slice(low * BLK, high * BLK)
        k_t[:, span] = dot(eye_hd, span_of(1, low, high), NT).astype(jnp.bfloat16)
        v_t[:, span] = dot(eye_hd, span_of(2, low, high), NT).astype(jnp.bfloat16)

    def folded(x):
        return x.reshape(x.shape[0] // 8, 8, x.shape[1])

    edge_low, edge_high = blocks // 4, 3 * blocks // 4

    def first_key(i):
        return edge_low if i >= edge_high else 0

    def scores(i, bound):
        low, high = first_key(i), i + 1
        s = dot(span_of(1, low, high), span_of(0, i, i + 1), NT) * logit_scale
        g = dot(span_of(2, low, high), span_of(3, i, i + 1), NT)
        pgrad[i, low * BLK : high * BLK, :] = g
        cols = i * BLK + lax.broadcasted_iota(jnp.int32, (1, BLK), 1)
        lowest = jnp.where(cols >= bound, bound, 0)
        top = None
        for j in range(low, high):
            part = s[(j - low) * BLK : (j - low + 1) * BLK]
            row = lax.broadcasted_iota(jnp.int32, (BLK, BLK), 0)
            if i >= edge_low and j < edge_high:
                part = jnp.where(row >= lowest - j * BLK, part, HIDE)
            if j == i:
                part = jnp.where(
                    row <= lax.broadcasted_iota(jnp.int32, (BLK, BLK), 1), part, HIDE
                )
            logit[i, j * BLK : (j + 1) * BLK, :] = part
            part = jnp.max(folded(part), axis=0)
            top = part if top is None else jnp.maximum(top, part)
        return jnp.max(top, axis=0, keepdims=True)

    def settle(i, top):
        total = delta = jnp.zeros((8, BLK), jnp.float32)
        for j in range(first_key(i), i + 1):
            span = slice(j * BLK, (j + 1) * BLK)
            e = jnp.exp2(logit[i, span, :] - top)
            total = total + jnp.sum(folded(e), axis=0)
            delta = delta + jnp.sum(folded(e * pgrad[i, span, :]), axis=0)
        total = jnp.sum(total, axis=0, keepdims=True)
        delta = jnp.sum(delta, axis=0, keepdims=True) / total
        return top + jnp.log2(total), delta

    def gradients(i, norm, delta, gt):
        low, high = first_key(i), i + 1
        weights, grads = [], []
        for j in range(low, high):
            span = slice(j * BLK, (j + 1) * BLK)
            s = logit[i, span, :]
            p = jnp.exp2(s - norm)
            ds = p * (pgrad[i, span, :] - delta)
            gt = gt + jnp.sum(folded(ds * s), axis=0)
            weights.append(p.astype(jnp.bfloat16))
            grads.append(ds.astype(jnp.bfloat16))
        p, ds = jnp.concatenate(weights, axis=0), jnp.concatenate(grads, axis=0)
        dv = dot(p, span_of(3, i, i + 1), NN)
        dk = dot(ds, span_of(0, i, i + 1), NN)
        if low < i:
            span = slice(low * BLK, i * BLK)
            dv_acc[span, :] += dv[: (i - low) * BLK]
            dk_acc[span, :] += dk[: (i - low) * BLK]
        span = slice(i * BLK, high * BLK)
        dv_acc[span, :] = dv[(i - low) * BLK :]
        dk_acc[span, :] = dk[(i - low) * BLK :]
        span = slice(low * BLK, high * BLK)
        o = dot(v_t[:, span], p, NN).astype(jnp.bfloat16)
        dq = (dot(k_t[:, span], ds, NN) * scale).astype(jnp.bfloat16)
        put(0, i, dot(eye_blk, o, NT))
        put(1, i, dot(eye_blk, dq, NT))
        return gt

    loads[0].wait()
    turn(0, group)
    tops = {0: scores(0, shards * rows)}
    gt = jnp.zeros((8, BLK), jnp.float32)
    bound = None
    for i in range(blocks):
        if i + 1 == group:
            loads[1].wait()
            ids = held[:, 4 * rows :, :].astype(jnp.float32)
            bound = shards * rows - (jnp.sum(ids) * (1.0 / PAD)).astype(jnp.int32)
            turn(group, blocks)
        if i + 1 < blocks:
            tops[i + 1] = scores(i + 1, shards * rows if bound is None else bound)
        norm, delta = settle(i, tops[i])
        gt = gradients(i, norm, delta, gt)
        if (i + 1) % group == 0:
            store(i + 1 - group, i + 1, 0).start()
    for i in range(blocks):
        span = slice(i * BLK, (i + 1) * BLK)
        put(2, i, dk_acc[span, :] * scale)
        put(3, i, dv_acc[span, :])
        if (i + 1) % group == 0:
            store(i + 1 - group, i + 1, 1).start()
    gt_ref[0] = jnp.sum(gt) / (temper * LOG2E)
    for first in range(0, blocks, group):
        store(first, first + group, 0).wait()
        store(first, first + group, 1).wait()


def vmem_spec():
    return pl.BlockSpec(memory_space=pltpu.VMEM)


def any_spec():
    return pl.BlockSpec(memory_space=pl.ANY)


def grant(mib):
    return pltpu.CompilerParams(vmem_limit_bytes=mib * MIB)


def body(queries, keys, values, cotangent, history, temper):
    _, rows, heads, hd = queries.shape
    shards = lax.axis_size("ctx")
    blocks = shards * rows // BLK
    low, f32 = jnp.bfloat16, jnp.float32

    send = pl.pallas_call(
        pack_body,
        out_shape=jax.ShapeDtypeStruct((heads, 4 * rows + PAD, hd), low),
        in_specs=[any_spec()] * 4 + [vmem_spec()],
        out_specs=any_spec(),
        scratch_shapes=[
            pltpu.VMEM((4, rows, heads, hd), low),
            pltpu.VMEM((2, rows * heads, hd), f32),
            pltpu.VMEM((heads, 4 * rows + PAD, hd), low),
            pltpu.SemaphoreType.DMA((4,)),
            pltpu.SemaphoreType.DMA((4,)),
        ],
        compiler_params=grant(56),
    )(queries[0], keys[0], values[0], cotangent[0], history)
    recv = lax.all_to_all(send, "ctx", split_axis=0, concat_axis=0, tiled=True)
    results, gt = pl.pallas_call(
        attend_body,
        out_shape=(
            jax.ShapeDtypeStruct((shards, 4 * rows, hd), low),
            jax.ShapeDtypeStruct((1,), f32),
        ),
        in_specs=[pl.BlockSpec(memory_space=pltpu.SMEM), any_spec()],
        out_specs=(any_spec(), pl.BlockSpec(memory_space=pltpu.SMEM)),
        scratch_shapes=[
            pltpu.VMEM((shards, 4 * rows + PAD, hd), low),
            pltpu.VMEM((shards, 4 * rows, hd), low),
            pltpu.VMEM((blocks, blocks * BLK, BLK), f32),
            pltpu.VMEM((blocks, blocks * BLK, BLK), f32),
            pltpu.VMEM((hd, blocks * BLK), low),
            pltpu.VMEM((hd, blocks * BLK), low),
            pltpu.VMEM((blocks * BLK, hd), f32),
            pltpu.VMEM((blocks * BLK, hd), f32),
            pltpu.SemaphoreType.DMA((2,)),
            pltpu.SemaphoreType.DMA((2, 4)),
        ],
        compiler_params=grant(60),
    )(temper, recv)
    back = lax.all_to_all(results, "ctx", split_axis=0, concat_axis=0, tiled=True)
    exp_size = lax.axis_size("exp")
    step = 1
    while step < exp_size:
        gt = gt + lax.ppermute(gt, "exp", [(n, (n + step) % exp_size) for n in range(exp_size)])
        step *= 2
    outs = pl.pallas_call(
        unpack_body,
        out_shape=[jax.ShapeDtypeStruct((rows, heads, hd), low)] * 4,
        in_specs=[any_spec()],
        out_specs=[any_spec()] * 4,
        scratch_shapes=[
            pltpu.VMEM((heads, 4 * rows, hd), low),
            pltpu.VMEM((2, rows * heads, hd), f32),
            pltpu.VMEM((4, rows, heads, hd), low),
            pltpu.SemaphoreType.DMA((4,)),
            pltpu.SemaphoreType.DMA((4,)),
        ],
        compiler_params=grant(16),
    )(back)
    attn_out, grad_q, grad_k, grad_v = [part[None] for part in outs]
    return attn_out, grad_q, grad_k, grad_v, gt


def solution(mesh):
    placed = P("exp", "ctx", None, None)
    return jax.shard_map(
        body,
        mesh=mesh,
        in_specs=(placed, placed, placed, placed, P("exp", "ctx"), P()),
        out_specs=(placed, placed, placed, placed, P("ctx")),
        check_vma=False,
    )
```

```python
import functools

import jax
import jax.numpy as jnp
from jax import lax
from jax.experimental import pallas as pl
from jax.experimental.pallas import tpu as pltpu
from jax.sharding import PartitionSpec as P

NT = (((1,), (1,)), ((), ()))
NN = (((1,), (0,)), ((), ()))
LOG2E = 1.4426950408889634
HIDE = -1e30
BLK = 512
PAD = 16
PARTS = 2
MIB = 1024 * 1024


def dot(a, b, dims):
    return lax.dot_general(a, b, dims, preferred_element_type=jnp.float32)


def pack_body(q_hbm, k_hbm, v_hbm, c_hbm, hist_ref, out_hbm, held, wide, packed, in_sem, out_sem):
    _, rows, heads, hd = held.shape
    size = rows // PARTS
    loads, stores = [], []
    for stage in range(4 * PARTS):
        place, span = stage // PARTS, pl.ds(stage % PARTS * size, size)
        ref = (q_hbm, k_hbm, v_hbm, c_hbm)[place]
        load = pltpu.make_async_copy(ref.at[span], held.at[place, span], in_sem.at[stage])
        load.start()
        loads.append(load)
    ids = jnp.broadcast_to(hist_ref[...].astype(jnp.float32), (PAD, rows)).astype(jnp.bfloat16)
    for head in range(heads):
        packed[head, 4 * rows :, :] = ids
    for stage, load in enumerate(loads):
        load.wait()
        place, first, slot = stage // PARTS, stage % PARTS * size, stage % 4
        part = held[place, first : first + size]
        wide[slot] = part.astype(jnp.float32).reshape(size * heads, hd)
        for head in range(heads):
            part = wide[slot, pl.ds(head, size, stride=heads), :]
            packed[head, stage * size : (stage + 1) * size, :] = part.astype(jnp.bfloat16)
        span = pl.ds(stage * size, size if stage + 1 < len(loads) else size + PAD)
        store = pltpu.make_async_copy(
            packed.at[:, span, :], out_hbm.at[:, span, :], out_sem.at[stage]
        )
        store.start()
        stores.append(store)
    for store in stores:
        store.wait()


def unpack_body(in_hbm, a_hbm, b_hbm, c_hbm, d_hbm, held, wide, packed, in_sem, out_sem):
    _, rows, heads, hd = packed.shape
    size = rows // PARTS
    loads, stores = [], []
    for stage in range(4 * PARTS):
        span = pl.ds(stage * size, size)
        load = pltpu.make_async_copy(
            in_hbm.at[:, span, :], held.at[:, span, :], in_sem.at[stage]
        )
        load.start()
        loads.append(load)
    for stage, load in enumerate(loads):
        load.wait()
        place, span, slot = stage // PARTS, pl.ds(stage % PARTS * size, size), stage % 4
        for head in range(heads):
            part = held[head, stage * size : (stage + 1) * size, :]
            wide[slot, pl.ds(head, size, stride=heads), :] = part.astype(jnp.float32)
        packed[place, span] = wide[slot].reshape(size, heads, hd).astype(jnp.bfloat16)
        ref = (a_hbm, b_hbm, c_hbm, d_hbm)[place]
        store = pltpu.make_async_copy(packed.at[place, span], ref.at[span], out_sem.at[stage])
        store.start()
        stores.append(store)
    for store in stores:
        store.wait()


def attend_body(
    temper_ref,
    in_hbm,
    out_hbm,
    gt_ref,
    held,
    ids,
    done,
    logit,
    pgrad,
    k_t,
    v_t,
    dk_acc,
    dv_acc,
    o_acc,
    dq_acc,
    in_sem,
    out_sem,
):
    shards, rows, hd = held.shape[0], held.shape[1] // 4, held.shape[2]
    per = BLK // rows
    blocks = shards // per
    half = BLK // 2
    data = pl.ds(0, 4 * rows)

    def load(block):
        span = pl.ds(block * per, per)
        return pltpu.make_async_copy(
            in_hbm.at[span, data, :], held.at[span, data, :], in_sem.at[block]
        )

    def store(block, kind):
        span, part = pl.ds(block * per, per), pl.ds(2 * kind * rows, 2 * rows)
        return pltpu.make_async_copy(
            done.at[span, part, :], out_hbm.at[span, part, :], out_sem.at[kind, block]
        )

    load_ids = pltpu.make_async_copy(in_hbm.at[:, pl.ds(4 * rows, PAD), :], ids, in_sem.at[blocks])
    load_ids.start()
    for block in range(blocks):
        load(block).start()
    temper = temper_ref[lax.axis_index("ctx")]
    scale = temper * hd ** (-0.5)
    logit_scale = scale * LOG2E
    load_ids.wait()
    bound = shards * rows - (jnp.sum(ids[...].astype(jnp.float32)) * (1.0 / PAD)).astype(jnp.int32)

    def rows_of(place, block):
        part = held[pl.ds(block * per, per), place * rows : (place + 1) * rows, :]
        return part.reshape(BLK, hd)

    def identity(size):
        return (
            lax.broadcasted_iota(jnp.int32, (size, size), 0)
            == lax.broadcasted_iota(jnp.int32, (size, size), 1)
        ).astype(jnp.bfloat16)

    eye_hd = identity(hd)
    eye_half = identity(half)

    def turned(part):
        return dot(eye_hd, part, NT).astype(jnp.bfloat16)

    def put(place, block, value):
        value = value.astype(jnp.bfloat16)
        value = jnp.concatenate(
            [dot(eye_half, value[:, n * half : (n + 1) * half], NT) for n in range(2)], axis=0
        )
        done[pl.ds(block * per, per), place * rows : (place + 1) * rows, :] = value.astype(
            jnp.bfloat16
        ).reshape(per, rows, hd)

    def folded(x):
        return x.reshape(x.shape[0] // 8, 8, x.shape[1])

    def query_block(i, gt):
        load(i).wait()
        q_i, k_i, v_i, c_i = [rows_of(place, i) for place in range(4)]
        k_t[i] = turned(k_i)
        v_t[i] = turned(v_i)
        q_t, c_t = turned(q_i), turned(c_i)
        dk_acc[i] = jnp.zeros((hd, BLK), jnp.float32)
        dv_acc[i] = jnp.zeros((hd, BLK), jnp.float32)
        first_i = i * BLK
        cols = first_i + lax.broadcasted_iota(jnp.int32, (1, BLK), 1)
        low = jnp.where(cols >= bound, bound, 0)
        start = jnp.where(first_i >= bound, bound // BLK, 0)

        def scan_keys(j, carry):
            top, total, delta = carry
            first_j = j * BLK
            s = dot(rows_of(1, j), q_i, NT) * logit_scale
            row = lax.broadcasted_iota(jnp.int32, (BLK, BLK), 0)
            s = jnp.where((row <= cols - first_j) & (row >= low - first_j), s, HIDE)
            logit[j] = s
            s = folded(s)
            g = dot(rows_of(2, j), c_i, NT)
            pgrad[j] = g
            new_top = jnp.maximum(top, jnp.max(s, axis=0))
            keep = jnp.exp2(top - new_top)
            e = jnp.exp2(s - new_top[None])
            total = total * keep + jnp.sum(e, axis=0)
            delta = delta * keep + jnp.sum(e * folded(g), axis=0)
            return new_top, total, delta

        zero = jnp.zeros((8, BLK), jnp.float32)
        top, total, delta = lax.fori_loop(
            start, i + 1, scan_keys, (jnp.full((8, BLK), HIDE, jnp.float32), zero, zero)
        )
        top_all = jnp.max(top, axis=0, keepdims=True)
        part = jnp.exp2(top - top_all)
        total = jnp.sum(total * part, axis=0, keepdims=True)
        delta = jnp.sum(delta * part, axis=0, keepdims=True) / total
        norm = top_all + jnp.log2(total)
        o_acc[...] = jnp.zeros((hd, BLK), jnp.float32)
        dq_acc[...] = jnp.zeros((hd, BLK), jnp.float32)

        def gradients(j, gt):
            s = logit[j]
            p = jnp.exp2(s - norm)
            ds = p * (pgrad[j] - delta)
            gt = gt + jnp.sum(folded(ds * s), axis=0)
            p, ds = p.astype(jnp.bfloat16), ds.astype(jnp.bfloat16)
            dv_acc[j] += dot(c_t, p, NT)
            dk_acc[j] += dot(q_t, ds, NT)
            o_acc[...] += dot(v_t[j], p, NN)
            dq_acc[...] += dot(k_t[j], ds, NN)
            return gt

        gt = lax.fori_loop(start, i + 1, gradients, gt)
        put(0, i, o_acc[...])
        put(1, i, dq_acc[...] * scale)
        store(i, 0).start()
        return gt

    gt = lax.fori_loop(0, blocks, query_block, jnp.zeros((8, BLK), jnp.float32))
    for block in range(blocks):
        put(2, block, dk_acc[block] * scale)
        put(3, block, dv_acc[block])
        store(block, 1).start()
    gt_ref[0] = jnp.sum(gt) / (temper * LOG2E)
    for block in range(blocks):
        store(block, 0).wait()
        store(block, 1).wait()


def vmem_spec():
    return pl.BlockSpec(memory_space=pltpu.VMEM)


def any_spec():
    return pl.BlockSpec(memory_space=pl.ANY)


def grant(mib):
    return pltpu.CompilerParams(vmem_limit_bytes=mib * MIB)


def body(queries, keys, values, cotangent, history, temper):
    _, rows, heads, hd = queries.shape
    shards = lax.axis_size("ctx")
    blocks = shards * rows // BLK
    low, f32 = jnp.bfloat16, jnp.float32

    send = pl.pallas_call(
        pack_body,
        out_shape=jax.ShapeDtypeStruct((heads, 4 * rows + PAD, hd), low),
        in_specs=[any_spec()] * 4 + [vmem_spec()],
        out_specs=any_spec(),
        scratch_shapes=[
            pltpu.VMEM((4, rows, heads, hd), low),
            pltpu.VMEM((4, rows // PARTS * heads, hd), f32),
            pltpu.VMEM((heads, 4 * rows + PAD, hd), low),
            pltpu.SemaphoreType.DMA((4 * PARTS,)),
            pltpu.SemaphoreType.DMA((4 * PARTS,)),
        ],
        compiler_params=grant(56),
    )(queries[0], keys[0], values[0], cotangent[0], history)
    recv = lax.all_to_all(send, "ctx", split_axis=0, concat_axis=0, tiled=True)
    results, gt = pl.pallas_call(
        attend_body,
        out_shape=(
            jax.ShapeDtypeStruct((shards, 4 * rows, hd), low),
            jax.ShapeDtypeStruct((1,), f32),
        ),
        in_specs=[pl.BlockSpec(memory_space=pltpu.SMEM), any_spec()],
        out_specs=(any_spec(), pl.BlockSpec(memory_space=pltpu.SMEM)),
        scratch_shapes=[
            pltpu.VMEM((shards, 4 * rows, hd), low),
            pltpu.VMEM((shards, PAD, hd), low),
            pltpu.VMEM((shards, 4 * rows, hd), low),
            pltpu.VMEM((blocks, BLK, BLK), f32),
            pltpu.VMEM((blocks, BLK, BLK), f32),
            pltpu.VMEM((blocks, hd, BLK), low),
            pltpu.VMEM((blocks, hd, BLK), low),
            pltpu.VMEM((blocks, hd, BLK), f32),
            pltpu.VMEM((blocks, hd, BLK), f32),
            pltpu.VMEM((hd, BLK), f32),
            pltpu.VMEM((hd, BLK), f32),
            pltpu.SemaphoreType.DMA((blocks + 1,)),
            pltpu.SemaphoreType.DMA((2, blocks)),
        ],
        compiler_params=grant(60),
    )(temper, recv)
    back = lax.all_to_all(results, "ctx", split_axis=0, concat_axis=0, tiled=True)
    exp_size = lax.axis_size("exp")
    step = 1
    while step < exp_size:
        gt = gt + lax.ppermute(gt, "exp", [(n, (n + step) % exp_size) for n in range(exp_size)])
        step *= 2
    outs = pl.pallas_call(
        unpack_body,
        out_shape=[jax.ShapeDtypeStruct((rows, heads, hd), low)] * 4,
        in_specs=[any_spec()],
        out_specs=[any_spec()] * 4,
        scratch_shapes=[
            pltpu.VMEM((heads, 4 * rows, hd), low),
            pltpu.VMEM((4, rows // PARTS * heads, hd), f32),
            pltpu.VMEM((4, rows, heads, hd), low),
            pltpu.SemaphoreType.DMA((4 * PARTS,)),
            pltpu.SemaphoreType.DMA((4 * PARTS,)),
        ],
        compiler_params=grant(16),
    )(back)
    attn_out, grad_q, grad_k, grad_v = [part[None] for part in outs]
    return attn_out, grad_q, grad_k, grad_v, gt


def solution(mesh):
    placed = P("exp", "ctx", None, None)
    return jax.shard_map(
        body,
        mesh=mesh,
        in_specs=(placed, placed, placed, placed, P("exp", "ctx"), P()),
        out_specs=(placed, placed, placed, placed, P("ctx")),
        check_vma=False,
    )
```

```python
import functools

import jax
import jax.numpy as jnp
from jax import lax
from jax.experimental import pallas as pl
from jax.experimental.pallas import tpu as pltpu
from jax.sharding import PartitionSpec as P

NT = (((1,), (1,)), ((), ()))
NN = (((1,), (0,)), ((), ()))
TN = (((0,), (0,)), ((), ()))
LOG2E = 1.4426950408889634
HIDE = -1e30
BLK = 512
PAD = 16
PARTS = 2
MIB = 1024 * 1024


def dot(a, b, dims):
    return lax.dot_general(a, b, dims, preferred_element_type=jnp.float32)


def pack_body(q_hbm, k_hbm, v_hbm, c_hbm, hist_ref, out_hbm, held, wide, packed, in_sem, out_sem):
    _, rows, heads, hd = held.shape
    size = rows // PARTS
    loads, stores = [], []
    for stage in range(4 * PARTS):
        place, span = stage // PARTS, pl.ds(stage % PARTS * size, size)
        ref = (q_hbm, k_hbm, v_hbm, c_hbm)[place]
        load = pltpu.make_async_copy(ref.at[span], held.at[place, span], in_sem.at[stage])
        load.start()
        loads.append(load)
    ids = jnp.broadcast_to(hist_ref[...].astype(jnp.float32), (PAD, rows)).astype(jnp.bfloat16)
    for head in range(heads):
        packed[head, 4 * rows :, :] = ids
    for stage, load in enumerate(loads):
        load.wait()
        place, first, slot = stage // PARTS, stage % PARTS * size, stage % 4
        part = held[place, first : first + size]
        wide[slot] = part.astype(jnp.float32).reshape(size * heads, hd)
        for head in range(heads):
            part = wide[slot, pl.ds(head, size, stride=heads), :]
            packed[head, stage * size : (stage + 1) * size, :] = part.astype(jnp.bfloat16)
        span = pl.ds(stage * size, size if stage + 1 < len(loads) else size + PAD)
        store = pltpu.make_async_copy(
            packed.at[:, span, :], out_hbm.at[:, span, :], out_sem.at[stage]
        )
        store.start()
        stores.append(store)
    for store in stores:
        store.wait()


def unpack_body(in_hbm, a_hbm, b_hbm, c_hbm, d_hbm, held, wide, packed, in_sem, out_sem):
    _, rows, heads, hd = packed.shape
    size = rows // PARTS
    loads, stores = [], []
    for stage in range(4 * PARTS):
        span = pl.ds(stage * size, size)
        load = pltpu.make_async_copy(
            in_hbm.at[:, span, :], held.at[:, span, :], in_sem.at[stage]
        )
        load.start()
        loads.append(load)
    for stage, load in enumerate(loads):
        load.wait()
        place, span, slot = stage // PARTS, pl.ds(stage % PARTS * size, size), stage % 4
        for head in range(heads):
            part = held[head, stage * size : (stage + 1) * size, :]
            wide[slot, pl.ds(head, size, stride=heads), :] = part.astype(jnp.float32)
        packed[place, span] = wide[slot].reshape(size, heads, hd).astype(jnp.bfloat16)
        ref = (a_hbm, b_hbm, c_hbm, d_hbm)[place]
        store = pltpu.make_async_copy(packed.at[place, span], ref.at[span], out_sem.at[stage])
        store.start()
        stores.append(store)
    for store in stores:
        store.wait()


def attend_body(
    temper_ref,
    in_hbm,
    out_hbm,
    gt_ref,
    held,
    ids,
    done,
    logit,
    pgrad,
    dk_acc,
    dv_acc,
    o_acc,
    dq_acc,
    in_sem,
    out_sem,
):
    shards, rows, hd = held.shape[0], held.shape[1] // 4, held.shape[2]
    per = BLK // rows
    blocks = shards // per
    data = pl.ds(0, 4 * rows)

    def load(block):
        span = pl.ds(block * per, per)
        return pltpu.make_async_copy(
            in_hbm.at[span, data, :], held.at[span, data, :], in_sem.at[block]
        )

    def store(block, kind):
        span, part = pl.ds(block * per, per), pl.ds(2 * kind * rows, 2 * rows)
        return pltpu.make_async_copy(
            done.at[span, part, :], out_hbm.at[span, part, :], out_sem.at[kind, block]
        )

    load_ids = pltpu.make_async_copy(in_hbm.at[:, pl.ds(4 * rows, PAD), :], ids, in_sem.at[blocks])
    load_ids.start()
    for block in range(blocks):
        load(block).start()
    temper = temper_ref[lax.axis_index("ctx")]
    scale = temper * hd ** (-0.5)
    logit_scale = scale * LOG2E
    load_ids.wait()
    bound = shards * rows - (jnp.sum(ids[...].astype(jnp.float32)) * (1.0 / PAD)).astype(jnp.int32)

    def rows_of(place, block):
        part = held[pl.ds(block * per, per), place * rows : (place + 1) * rows, :]
        return part.reshape(BLK, hd)

    def put(place, block, value):
        done[pl.ds(block * per, per), place * rows : (place + 1) * rows, :] = value.astype(
            jnp.bfloat16
        ).reshape(per, rows, hd)

    def folded(x):
        return x.reshape(x.shape[0] // 8, 8, x.shape[1])

    def query_block(i, gt):
        load(i).wait()
        q_i, c_i = rows_of(0, i), rows_of(3, i)
        dk_acc[i] = jnp.zeros((BLK, hd), jnp.float32)
        dv_acc[i] = jnp.zeros((BLK, hd), jnp.float32)
        first_i = i * BLK
        cols = first_i + lax.broadcasted_iota(jnp.int32, (1, BLK), 1)
        low = jnp.where(cols >= bound, bound, 0)
        start = jnp.where(first_i >= bound, bound // BLK, 0)

        def scan_keys(j, carry):
            top, total, delta = carry
            first_j = j * BLK
            s = dot(rows_of(1, j), q_i, NT) * logit_scale
            row = lax.broadcasted_iota(jnp.int32, (BLK, BLK), 0)
            s = jnp.where((row <= cols - first_j) & (row >= low - first_j), s, HIDE)
            logit[j] = s
            s = folded(s)
            g = dot(rows_of(2, j), c_i, NT)
            pgrad[j] = g
            new_top = jnp.maximum(top, jnp.max(s, axis=0))
            keep = jnp.exp2(top - new_top)
            e = jnp.exp2(s - new_top[None])
            total = total * keep + jnp.sum(e, axis=0)
            delta = delta * keep + jnp.sum(e * folded(g), axis=0)
            return new_top, total, delta

        zero = jnp.zeros((8, BLK), jnp.float32)
        top, total, delta = lax.fori_loop(
            start, i + 1, scan_keys, (jnp.full((8, BLK), HIDE, jnp.float32), zero, zero)
        )
        top_all = jnp.max(top, axis=0, keepdims=True)
        part = jnp.exp2(top - top_all)
        total = jnp.sum(total * part, axis=0, keepdims=True)
        delta = jnp.sum(delta * part, axis=0, keepdims=True) / total
        norm = top_all + jnp.log2(total)
        o_acc[...] = jnp.zeros((BLK, hd), jnp.float32)
        dq_acc[...] = jnp.zeros((BLK, hd), jnp.float32)

        def gradients(j, gt):
            s = logit[j]
            p = jnp.exp2(s - norm)
            ds = p * (pgrad[j] - delta)
            gt = gt + jnp.sum(folded(ds * s), axis=0)
            p, ds = p.astype(jnp.bfloat16), ds.astype(jnp.bfloat16)
            dv_acc[j] += dot(p, c_i, NN)
            dk_acc[j] += dot(ds, q_i, NN)
            o_acc[...] += dot(p, rows_of(2, j), TN)
            dq_acc[...] += dot(ds, rows_of(1, j), TN)
            return gt

        gt = lax.fori_loop(start, i + 1, gradients, gt)
        put(0, i, o_acc[...])
        put(1, i, dq_acc[...] * scale)
        store(i, 0).start()
        return gt

    gt = lax.fori_loop(0, blocks, query_block, jnp.zeros((8, BLK), jnp.float32))
    for block in range(blocks):
        put(2, block, dk_acc[block] * scale)
        put(3, block, dv_acc[block])
        store(block, 1).start()
    gt_ref[0] = jnp.sum(gt) / (temper * LOG2E)
    for block in range(blocks):
        store(block, 0).wait()
        store(block, 1).wait()


def vmem_spec():
    return pl.BlockSpec(memory_space=pltpu.VMEM)


def any_spec():
    return pl.BlockSpec(memory_space=pl.ANY)


def grant(mib):
    return pltpu.CompilerParams(vmem_limit_bytes=mib * MIB)


def body(queries, keys, values, cotangent, history, temper):
    _, rows, heads, hd = queries.shape
    shards = lax.axis_size("ctx")
    blocks = shards * rows // BLK
    low, f32 = jnp.bfloat16, jnp.float32

    send = pl.pallas_call(
        pack_body,
        out_shape=jax.ShapeDtypeStruct((heads, 4 * rows + PAD, hd), low),
        in_specs=[any_spec()] * 4 + [vmem_spec()],
        out_specs=any_spec(),
        scratch_shapes=[
            pltpu.VMEM((4, rows, heads, hd), low),
            pltpu.VMEM((4, rows // PARTS * heads, hd), f32),
            pltpu.VMEM((heads, 4 * rows + PAD, hd), low),
            pltpu.SemaphoreType.DMA((4 * PARTS,)),
            pltpu.SemaphoreType.DMA((4 * PARTS,)),
        ],
        compiler_params=grant(56),
    )(queries[0], keys[0], values[0], cotangent[0], history)
    recv = lax.all_to_all(send, "ctx", split_axis=0, concat_axis=0, tiled=True)
    results, gt = pl.pallas_call(
        attend_body,
        out_shape=(
            jax.ShapeDtypeStruct((shards, 4 * rows, hd), low),
            jax.ShapeDtypeStruct((1,), f32),
        ),
        in_specs=[pl.BlockSpec(memory_space=pltpu.SMEM), any_spec()],
        out_specs=(any_spec(), pl.BlockSpec(memory_space=pltpu.SMEM)),
        scratch_shapes=[
            pltpu.VMEM((shards, 4 * rows, hd), low),
            pltpu.VMEM((shards, PAD, hd), low),
            pltpu.VMEM((shards, 4 * rows, hd), low),
            pltpu.VMEM((blocks, BLK, BLK), f32),
            pltpu.VMEM((blocks, BLK, BLK), f32),
            pltpu.VMEM((blocks, BLK, hd), f32),
            pltpu.VMEM((blocks, BLK, hd), f32),
            pltpu.VMEM((BLK, hd), f32),
            pltpu.VMEM((BLK, hd), f32),
            pltpu.SemaphoreType.DMA((blocks + 1,)),
            pltpu.SemaphoreType.DMA((2, blocks)),
        ],
        compiler_params=grant(60),
    )(temper, recv)
    back = lax.all_to_all(results, "ctx", split_axis=0, concat_axis=0, tiled=True)
    exp_size = lax.axis_size("exp")
    step = 1
    while step < exp_size:
        gt = gt + lax.ppermute(gt, "exp", [(n, (n + step) % exp_size) for n in range(exp_size)])
        step *= 2
    outs = pl.pallas_call(
        unpack_body,
        out_shape=[jax.ShapeDtypeStruct((rows, heads, hd), low)] * 4,
        in_specs=[any_spec()],
        out_specs=[any_spec()] * 4,
        scratch_shapes=[
            pltpu.VMEM((heads, 4 * rows, hd), low),
            pltpu.VMEM((4, rows // PARTS * heads, hd), f32),
            pltpu.VMEM((4, rows, heads, hd), low),
            pltpu.SemaphoreType.DMA((4 * PARTS,)),
            pltpu.SemaphoreType.DMA((4 * PARTS,)),
        ],
        compiler_params=grant(16),
    )(back)
    attn_out, grad_q, grad_k, grad_v = [part[None] for part in outs]
    return attn_out, grad_q, grad_k, grad_v, gt


def solution(mesh):
    placed = P("exp", "ctx", None, None)
    return jax.shard_map(
        body,
        mesh=mesh,
        in_specs=(placed, placed, placed, placed, P("exp", "ctx"), P()),
        out_specs=(placed, placed, placed, placed, P("ctx")),
        check_vma=False,
    )
```

```python
import functools

import jax
import jax.numpy as jnp
from jax import lax
from jax.experimental import pallas as pl
from jax.experimental.pallas import tpu as pltpu
from jax.sharding import PartitionSpec as P

NT = (((1,), (1,)), ((), ()))
NN = (((1,), (0,)), ((), ()))
TN = (((0,), (0,)), ((), ()))
LOG2E = 1.4426950408889634
HIDE = -1e30
BLK = 256
PAD = 16
PARTS = 2
MIB = 1024 * 1024


def dot(a, b, dims):
    return lax.dot_general(a, b, dims, preferred_element_type=jnp.float32)


def pack_body(q_hbm, k_hbm, v_hbm, c_hbm, hist_ref, out_hbm, held, wide, packed, in_sem, out_sem):
    _, rows, heads, hd = held.shape
    size = rows // PARTS
    loads, stores = [], []
    for stage in range(4 * PARTS):
        place, span = stage // PARTS, pl.ds(stage % PARTS * size, size)
        ref = (q_hbm, k_hbm, v_hbm, c_hbm)[place]
        load = pltpu.make_async_copy(ref.at[span], held.at[place, span], in_sem.at[stage])
        load.start()
        loads.append(load)
    ids = jnp.broadcast_to(hist_ref[...].astype(jnp.float32), (PAD, rows)).astype(jnp.bfloat16)
    for head in range(heads):
        packed[head, 4 * rows :, :] = ids
    for stage, load in enumerate(loads):
        load.wait()
        place, first, slot = stage // PARTS, stage % PARTS * size, stage % 4
        part = held[place, first : first + size]
        wide[slot] = part.astype(jnp.float32).reshape(size * heads, hd)
        for head in range(heads):
            part = wide[slot, pl.ds(head, size, stride=heads), :]
            packed[head, stage * size : (stage + 1) * size, :] = part.astype(jnp.bfloat16)
        span = pl.ds(stage * size, size if stage + 1 < len(loads) else size + PAD)
        store = pltpu.make_async_copy(
            packed.at[:, span, :], out_hbm.at[:, span, :], out_sem.at[stage]
        )
        store.start()
        stores.append(store)
    for store in stores:
        store.wait()


def unpack_body(in_hbm, a_hbm, b_hbm, c_hbm, d_hbm, held, wide, packed, in_sem, out_sem):
    _, rows, heads, hd = packed.shape
    size = rows // PARTS
    loads, stores = [], []
    for stage in range(4 * PARTS):
        span = pl.ds(stage * size, size)
        load = pltpu.make_async_copy(
            in_hbm.at[:, span, :], held.at[:, span, :], in_sem.at[stage]
        )
        load.start()
        loads.append(load)
    for stage, load in enumerate(loads):
        load.wait()
        place, span, slot = stage // PARTS, pl.ds(stage % PARTS * size, size), stage % 4
        for head in range(heads):
            part = held[head, stage * size : (stage + 1) * size, :]
            wide[slot, pl.ds(head, size, stride=heads), :] = part.astype(jnp.float32)
        packed[place, span] = wide[slot].reshape(size, heads, hd).astype(jnp.bfloat16)
        ref = (a_hbm, b_hbm, c_hbm, d_hbm)[place]
        store = pltpu.make_async_copy(packed.at[place, span], ref.at[span], out_sem.at[stage])
        store.start()
        stores.append(store)
    for store in stores:
        store.wait()


def attend_body(
    temper_ref,
    in_hbm,
    out_hbm,
    gt_ref,
    held,
    done,
    logit,
    pgrad,
    v_t,
    dk_acc,
    dv_acc,
    in_sem,
    out_sem,
):
    shards, hd = held.shape[0], held.shape[2]
    rows = done.shape[1] // 4
    per = BLK // rows
    blocks = shards // per
    group = blocks // 4
    loads = [
        pltpu.make_async_copy(in_hbm.at[span], held.at[span], in_sem.at[n])
        for n, span in enumerate(
            (pl.ds(0, group * per), pl.ds(group * per, shards - group * per))
        )
    ]
    for load in loads:
        load.start()
    temper = temper_ref[lax.axis_index("ctx")]
    scale = temper * hd ** (-0.5)
    logit_scale = scale * LOG2E

    def identity(size):
        return (
            lax.broadcasted_iota(jnp.int32, (size, size), 0)
            == lax.broadcasted_iota(jnp.int32, (size, size), 1)
        ).astype(jnp.bfloat16)

    eye_hd = identity(hd)
    eye_blk = identity(BLK)

    def span_of(place, low, high):
        part = held[low * per : high * per, place * rows : (place + 1) * rows, :]
        return part.reshape((high - low) * BLK, hd)

    def put(place, block, value):
        done[block * per : (block + 1) * per, place * rows : (place + 1) * rows, :] = value.astype(
            jnp.bfloat16
        ).reshape(per, rows, hd)

    def store(first, last, kind):
        span, part = pl.ds(first * per, (last - first) * per), pl.ds(2 * kind * rows, 2 * rows)
        return pltpu.make_async_copy(
            done.at[span, part, :], out_hbm.at[span, part, :], out_sem.at[kind, first // group]
        )

    def turn(low, high):
        span = slice(low * BLK, high * BLK)
        v_t[:, span] = dot(eye_hd, span_of(2, low, high), NT).astype(jnp.bfloat16)

    def folded(x):
        return x.reshape(x.shape[0] // 8, 8, x.shape[1])

    edge_low, edge_high = blocks // 4, 3 * blocks // 4

    def first_key(i):
        return edge_low if i >= edge_high else 0

    def scores(i, bound):
        low, high = first_key(i), i + 1
        s = dot(span_of(1, low, high), span_of(0, i, i + 1), NT) * logit_scale
        g = dot(span_of(2, low, high), span_of(3, i, i + 1), NT)
        pgrad[i, low * BLK : high * BLK, :] = g
        cols = i * BLK + lax.broadcasted_iota(jnp.int32, (1, BLK), 1)
        lowest = jnp.where(cols >= bound, bound, 0)
        top = None
        for j in range(low, high):
            part = s[(j - low) * BLK : (j - low + 1) * BLK]
            row = lax.broadcasted_iota(jnp.int32, (BLK, BLK), 0)
            if i >= edge_low and j < edge_high:
                part = jnp.where(row >= lowest - j * BLK, part, HIDE)
            if j == i:
                part = jnp.where(
                    row <= lax.broadcasted_iota(jnp.int32, (BLK, BLK), 1), part, HIDE
                )
            logit[i, j * BLK : (j + 1) * BLK, :] = part
            part = jnp.max(folded(part), axis=0)
            top = part if top is None else jnp.maximum(top, part)
        return jnp.max(top, axis=0, keepdims=True)

    def settle(i, top):
        total = delta = jnp.zeros((8, BLK), jnp.float32)
        for j in range(first_key(i), i + 1):
            span = slice(j * BLK, (j + 1) * BLK)
            e = jnp.exp2(logit[i, span, :] - top)
            total = total + jnp.sum(folded(e), axis=0)
            delta = delta + jnp.sum(folded(e * pgrad[i, span, :]), axis=0)
        total = jnp.sum(total, axis=0, keepdims=True)
        delta = jnp.sum(delta, axis=0, keepdims=True) / total
        return top + jnp.log2(total), delta

    def gradients(i, norm, delta, gt):
        low, high = first_key(i), i + 1
        weights, grads = [], []
        for j in range(low, high):
            span = slice(j * BLK, (j + 1) * BLK)
            s = logit[i, span, :]
            p = jnp.exp2(s - norm)
            ds = p * (pgrad[i, span, :] - delta)
            gt = gt + jnp.sum(folded(ds * s), axis=0)
            weights.append(p.astype(jnp.bfloat16))
            grads.append(ds.astype(jnp.bfloat16))
        p, ds = jnp.concatenate(weights, axis=0), jnp.concatenate(grads, axis=0)
        dv = dot(p, span_of(3, i, i + 1), NN)
        dk = dot(ds, span_of(0, i, i + 1), NN)
        if low < i:
            span = slice(low * BLK, i * BLK)
            dv_acc[span, :] += dv[: (i - low) * BLK]
            dk_acc[span, :] += dk[: (i - low) * BLK]
        span = slice(i * BLK, high * BLK)
        dv_acc[span, :] = dv[(i - low) * BLK :]
        dk_acc[span, :] = dk[(i - low) * BLK :]
        span = slice(low * BLK, high * BLK)
        o = dot(v_t[:, span], p, NN).astype(jnp.bfloat16)
        dq = dot(ds, span_of(1, low, high), TN) * scale
        put(0, i, dot(eye_blk, o, NT))
        put(1, i, dq)
        return gt

    loads[0].wait()
    turn(0, group)
    tops = {0: scores(0, shards * rows)}
    gt = jnp.zeros((8, BLK), jnp.float32)
    bound = None
    for i in range(blocks):
        if i + 1 == group:
            loads[1].wait()
            ids = held[:, 4 * rows :, :].astype(jnp.float32)
            bound = shards * rows - (jnp.sum(ids) * (1.0 / PAD)).astype(jnp.int32)
            turn(group, blocks)
        if i + 1 < blocks:
            tops[i + 1] = scores(i + 1, shards * rows if bound is None else bound)
        norm, delta = settle(i, tops[i])
        gt = gradients(i, norm, delta, gt)
        if (i + 1) % group == 0:
            store(i + 1 - group, i + 1, 0).start()
    for i in range(blocks):
        span = slice(i * BLK, (i + 1) * BLK)
        put(2, i, dk_acc[span, :] * scale)
        put(3, i, dv_acc[span, :])
        if (i + 1) % group == 0:
            store(i + 1 - group, i + 1, 1).start()
    gt_ref[0] = jnp.sum(gt) / (temper * LOG2E)
    for first in range(0, blocks, group):
        store(first, first + group, 0).wait()
        store(first, first + group, 1).wait()


def vmem_spec():
    return pl.BlockSpec(memory_space=pltpu.VMEM)


def any_spec():
    return pl.BlockSpec(memory_space=pl.ANY)


def grant(mib):
    return pltpu.CompilerParams(vmem_limit_bytes=mib * MIB)


def body(queries, keys, values, cotangent, history, temper):
    _, rows, heads, hd = queries.shape
    shards = lax.axis_size("ctx")
    blocks = shards * rows // BLK
    low, f32 = jnp.bfloat16, jnp.float32

    send = pl.pallas_call(
        pack_body,
        out_shape=jax.ShapeDtypeStruct((heads, 4 * rows + PAD, hd), low),
        in_specs=[any_spec()] * 4 + [vmem_spec()],
        out_specs=any_spec(),
        scratch_shapes=[
            pltpu.VMEM((4, rows, heads, hd), low),
            pltpu.VMEM((4, rows // PARTS * heads, hd), f32),
            pltpu.VMEM((heads, 4 * rows + PAD, hd), low),
            pltpu.SemaphoreType.DMA((4 * PARTS,)),
            pltpu.SemaphoreType.DMA((4 * PARTS,)),
        ],
        compiler_params=grant(56),
    )(queries[0], keys[0], values[0], cotangent[0], history)
    recv = lax.all_to_all(send, "ctx", split_axis=0, concat_axis=0, tiled=True)
    results, gt = pl.pallas_call(
        attend_body,
        out_shape=(
            jax.ShapeDtypeStruct((shards, 4 * rows, hd), low),
            jax.ShapeDtypeStruct((1,), f32),
        ),
        in_specs=[pl.BlockSpec(memory_space=pltpu.SMEM), any_spec()],
        out_specs=(any_spec(), pl.BlockSpec(memory_space=pltpu.SMEM)),
        scratch_shapes=[
            pltpu.VMEM((shards, 4 * rows + PAD, hd), low),
            pltpu.VMEM((shards, 4 * rows, hd), low),
            pltpu.VMEM((blocks, blocks * BLK, BLK), f32),
            pltpu.VMEM((blocks, blocks * BLK, BLK), f32),
            pltpu.VMEM((hd, blocks * BLK), low),
            pltpu.VMEM((blocks * BLK, hd), f32),
            pltpu.VMEM((blocks * BLK, hd), f32),
            pltpu.SemaphoreType.DMA((2,)),
            pltpu.SemaphoreType.DMA((2, 4)),
        ],
        compiler_params=grant(60),
    )(temper, recv)
    back = lax.all_to_all(results, "ctx", split_axis=0, concat_axis=0, tiled=True)
    exp_size = lax.axis_size("exp")
    step = 1
    while step < exp_size:
        gt = gt + lax.ppermute(gt, "exp", [(n, (n + step) % exp_size) for n in range(exp_size)])
        step *= 2
    outs = pl.pallas_call(
        unpack_body,
        out_shape=[jax.ShapeDtypeStruct((rows, heads, hd), low)] * 4,
        in_specs=[any_spec()],
        out_specs=[any_spec()] * 4,
        scratch_shapes=[
            pltpu.VMEM((heads, 4 * rows, hd), low),
            pltpu.VMEM((4, rows // PARTS * heads, hd), f32),
            pltpu.VMEM((4, rows, heads, hd), low),
            pltpu.SemaphoreType.DMA((4 * PARTS,)),
            pltpu.SemaphoreType.DMA((4 * PARTS,)),
        ],
        compiler_params=grant(16),
    )(back)
    attn_out, grad_q, grad_k, grad_v = [part[None] for part in outs]
    return attn_out, grad_q, grad_k, grad_v, gt


def solution(mesh):
    placed = P("exp", "ctx", None, None)
    return jax.shard_map(
        body,
        mesh=mesh,
        in_specs=(placed, placed, placed, placed, P("exp", "ctx"), P()),
        out_specs=(placed, placed, placed, placed, P("ctx")),
        check_vma=False,
    )
```

```python
import functools

import jax
import jax.numpy as jnp
from jax import lax
from jax.experimental import pallas as pl
from jax.experimental.pallas import tpu as pltpu
from jax.sharding import PartitionSpec as P

NT = (((1,), (1,)), ((), ()))
NN = (((1,), (0,)), ((), ()))
TN = (((0,), (0,)), ((), ()))
LOG2E = 1.4426950408889634
HIDE = -1e30
BLK = 256
PAD = 16
PARTS = 2
MIB = 1024 * 1024


def dot(a, b, dims):
    return lax.dot_general(a, b, dims, preferred_element_type=jnp.float32)


def pack_body(q_hbm, k_hbm, v_hbm, c_hbm, hist_ref, out_hbm, held, wide, packed, in_sem, out_sem):
    _, rows, heads, hd = held.shape
    size = rows // PARTS
    loads, stores = [], []
    for stage in range(4 * PARTS):
        place, span = stage // PARTS, pl.ds(stage % PARTS * size, size)
        ref = (q_hbm, k_hbm, v_hbm, c_hbm)[place]
        load = pltpu.make_async_copy(ref.at[span], held.at[place, span], in_sem.at[stage])
        load.start()
        loads.append(load)
    ids = jnp.broadcast_to(hist_ref[...].astype(jnp.float32), (PAD, rows)).astype(jnp.bfloat16)
    for head in range(heads):
        packed[head, 4 * rows :, :] = ids
    for stage, load in enumerate(loads):
        load.wait()
        place, first, slot = stage // PARTS, stage % PARTS * size, stage % 4
        part = held[place, first : first + size]
        wide[slot] = part.astype(jnp.float32).reshape(size * heads, hd)
        for head in range(heads):
            part = wide[slot, pl.ds(head, size, stride=heads), :]
            packed[head, stage * size : (stage + 1) * size, :] = part.astype(jnp.bfloat16)
        span = pl.ds(stage * size, size if stage + 1 < len(loads) else size + PAD)
        store = pltpu.make_async_copy(
            packed.at[:, span, :], out_hbm.at[:, span, :], out_sem.at[stage]
        )
        store.start()
        stores.append(store)
    for store in stores:
        store.wait()


def unpack_body(in_hbm, a_hbm, b_hbm, c_hbm, d_hbm, held, wide, packed, in_sem, out_sem):
    _, rows, heads, hd = packed.shape
    size = rows // PARTS
    loads, stores = [], []
    for stage in range(4 * PARTS):
        span = pl.ds(stage * size, size)
        load = pltpu.make_async_copy(
            in_hbm.at[:, span, :], held.at[:, span, :], in_sem.at[stage]
        )
        load.start()
        loads.append(load)
    for stage, load in enumerate(loads):
        load.wait()
        place, span, slot = stage // PARTS, pl.ds(stage % PARTS * size, size), stage % 4
        for head in range(heads):
            part = held[head, stage * size : (stage + 1) * size, :]
            wide[slot, pl.ds(head, size, stride=heads), :] = part.astype(jnp.float32)
        packed[place, span] = wide[slot].reshape(size, heads, hd).astype(jnp.bfloat16)
        ref = (a_hbm, b_hbm, c_hbm, d_hbm)[place]
        store = pltpu.make_async_copy(packed.at[place, span], ref.at[span], out_sem.at[stage])
        store.start()
        stores.append(store)
    for store in stores:
        store.wait()


def attend_body(
    temper_ref,
    in_hbm,
    out_hbm,
    gt_ref,
    held,
    done,
    logit,
    pgrad,
    v_t,
    dk_acc,
    dv_acc,
    in_sem,
    out_sem,
):
    shards, hd = held.shape[0], held.shape[2]
    rows = done.shape[1] // 4
    per = BLK // rows
    blocks = shards // per
    group = blocks // 4
    loads = [
        pltpu.make_async_copy(in_hbm.at[span], held.at[span], in_sem.at[n])
        for n, span in enumerate(
            (pl.ds(0, group * per), pl.ds(group * per, shards - group * per))
        )
    ]
    for load in loads:
        load.start()
    temper = temper_ref[lax.axis_index("ctx")]
    scale = temper * hd ** (-0.5)
    logit_scale = scale * LOG2E

    def identity(size):
        return (
            lax.broadcasted_iota(jnp.int32, (size, size), 0)
            == lax.broadcasted_iota(jnp.int32, (size, size), 1)
        ).astype(jnp.bfloat16)

    eye_hd = identity(hd)
    eye_blk = identity(BLK)

    def span_of(place, low, high):
        part = held[low * per : high * per, place * rows : (place + 1) * rows, :]
        return part.reshape((high - low) * BLK, hd)

    def put(place, block, value):
        done[block * per : (block + 1) * per, place * rows : (place + 1) * rows, :] = value.astype(
            jnp.bfloat16
        ).reshape(per, rows, hd)

    def store(first, last, kind):
        span, part = pl.ds(first * per, (last - first) * per), pl.ds(2 * kind * rows, 2 * rows)
        return pltpu.make_async_copy(
            done.at[span, part, :], out_hbm.at[span, part, :], out_sem.at[kind, first // group]
        )

    def turn(low, high):
        span = slice(low * BLK, high * BLK)
        v_t[:, span] = dot(eye_hd, span_of(2, low, high), NT).astype(jnp.bfloat16)

    def folded(x):
        return x.reshape(x.shape[0] // 8, 8, x.shape[1])

    edge_low, edge_high = blocks // 4, 3 * blocks // 4

    def first_key(i, edge):
        return edge if i > edge else 0

    def scores(i, edge, bound):
        low, high = first_key(i, edge), i + 1
        s = dot(span_of(1, low, high), span_of(0, i, i + 1), NT) * logit_scale
        g = dot(span_of(2, low, high), span_of(3, i, i + 1), NT)
        pgrad[i, low * BLK : high * BLK, :] = g
        cols = i * BLK + lax.broadcasted_iota(jnp.int32, (1, BLK), 1)
        lowest = jnp.where(cols >= bound, bound, 0)
        top = None
        for j in range(low, high):
            part = s[(j - low) * BLK : (j - low + 1) * BLK]
            row = lax.broadcasted_iota(jnp.int32, (BLK, BLK), 0)
            if i == edge or j == edge:
                part = jnp.where(row >= lowest - j * BLK, part, HIDE)
            if j == i:
                part = jnp.where(
                    row <= lax.broadcasted_iota(jnp.int32, (BLK, BLK), 1), part, HIDE
                )
            logit[i, j * BLK : (j + 1) * BLK, :] = part
            part = jnp.max(folded(part), axis=0)
            top = part if top is None else jnp.maximum(top, part)
        return jnp.max(top, axis=0, keepdims=True)

    def settle(i, edge, top):
        total = delta = jnp.zeros((8, BLK), jnp.float32)
        for j in range(first_key(i, edge), i + 1):
            span = slice(j * BLK, (j + 1) * BLK)
            e = jnp.exp2(logit[i, span, :] - top)
            total = total + jnp.sum(folded(e), axis=0)
            delta = delta + jnp.sum(folded(e * pgrad[i, span, :]), axis=0)
        total = jnp.sum(total, axis=0, keepdims=True)
        delta = jnp.sum(delta, axis=0, keepdims=True) / total
        return top + jnp.log2(total), delta

    def gradients(i, edge, norm, delta, gt):
        low, high = first_key(i, edge), i + 1
        weights, grads = [], []
        for j in range(low, high):
            span = slice(j * BLK, (j + 1) * BLK)
            s = logit[i, span, :]
            p = jnp.exp2(s - norm)
            ds = p * (pgrad[i, span, :] - delta)
            gt = gt + jnp.sum(folded(ds * s), axis=0)
            weights.append(p.astype(jnp.bfloat16))
            grads.append(ds.astype(jnp.bfloat16))
        p, ds = jnp.concatenate(weights, axis=0), jnp.concatenate(grads, axis=0)
        dv = dot(p, span_of(3, i, i + 1), NN)
        dk = dot(ds, span_of(0, i, i + 1), NN)
        if low < i:
            span = slice(low * BLK, i * BLK)
            dv_acc[span, :] += dv[: (i - low) * BLK]
            dk_acc[span, :] += dk[: (i - low) * BLK]
        span = slice(i * BLK, high * BLK)
        dv_acc[span, :] = dv[(i - low) * BLK :]
        dk_acc[span, :] = dk[(i - low) * BLK :]
        span = slice(low * BLK, high * BLK)
        o = dot(v_t[:, span], p, NN).astype(jnp.bfloat16)
        dq = dot(ds, span_of(1, low, high), TN) * scale
        put(0, i, dot(eye_blk, o, NT))
        put(1, i, dq)
        return gt

    def leave(first, last):
        for j in range(first, last):
            span = slice(j * BLK, (j + 1) * BLK)
            put(2, j, dk_acc[span, :] * scale)
            put(3, j, dv_acc[span, :])
            if (j + 1) % group == 0:
                store(j + 1 - group, j + 1, 1).start()

    loads[0].wait()
    turn(0, group)
    everything = shards * rows
    top = scores(0, edge_high, everything)
    next_top = scores(1, edge_high, everything)
    norm, delta = settle(0, edge_high, top)
    first_gt = gradients(0, edge_high, norm, delta, jnp.zeros((8, BLK), jnp.float32))
    loads[1].wait()
    ids = held[:, 4 * rows :, :].astype(jnp.float32)
    bound = everything - (jnp.sum(ids) * (1.0 / PAD)).astype(jnp.int32)
    turn(group, blocks)
    edge_at = jnp.clip(bound // BLK, edge_low, edge_high - 1)

    def rest(edge):
        gt, top, left = first_gt, next_top, 0
        for i in range(1, blocks):
            if i + 1 < blocks:
                following = scores(i + 1, edge, bound)
            norm, delta = settle(i, edge, top)
            top = following
            gt = gradients(i, edge, norm, delta, gt)
            if (i + 1) % group == 0:
                store(i + 1 - group, i + 1, 0).start()
            if i == edge:
                left = edge // group * group
                leave(0, left)
        leave(left, blocks)
        gt_ref[0] = jnp.sum(gt) / (temper * LOG2E)

    for edge in range(edge_low, edge_high):
        pl.when(edge_at == edge)(functools.partial(rest, edge))
    for first in range(0, blocks, group):
        store(first, first + group, 0).wait()
        store(first, first + group, 1).wait()


def vmem_spec():
    return pl.BlockSpec(memory_space=pltpu.VMEM)


def any_spec():
    return pl.BlockSpec(memory_space=pl.ANY)


def grant(mib):
    return pltpu.CompilerParams(vmem_limit_bytes=mib * MIB)


def body(queries, keys, values, cotangent, history, temper):
    _, rows, heads, hd = queries.shape
    shards = lax.axis_size("ctx")
    blocks = shards * rows // BLK
    low, f32 = jnp.bfloat16, jnp.float32

    send = pl.pallas_call(
        pack_body,
        out_shape=jax.ShapeDtypeStruct((heads, 4 * rows + PAD, hd), low),
        in_specs=[any_spec()] * 4 + [vmem_spec()],
        out_specs=any_spec(),
        scratch_shapes=[
            pltpu.VMEM((4, rows, heads, hd), low),
            pltpu.VMEM((4, rows // PARTS * heads, hd), f32),
            pltpu.VMEM((heads, 4 * rows + PAD, hd), low),
            pltpu.SemaphoreType.DMA((4 * PARTS,)),
            pltpu.SemaphoreType.DMA((4 * PARTS,)),
        ],
        compiler_params=grant(56),
    )(queries[0], keys[0], values[0], cotangent[0], history)
    recv = lax.all_to_all(send, "ctx", split_axis=0, concat_axis=0, tiled=True)
    results, gt = pl.pallas_call(
        attend_body,
        out_shape=(
            jax.ShapeDtypeStruct((shards, 4 * rows, hd), low),
            jax.ShapeDtypeStruct((1,), f32),
        ),
        in_specs=[pl.BlockSpec(memory_space=pltpu.SMEM), any_spec()],
        out_specs=(any_spec(), pl.BlockSpec(memory_space=pltpu.SMEM)),
        scratch_shapes=[
            pltpu.VMEM((shards, 4 * rows + PAD, hd), low),
            pltpu.VMEM((shards, 4 * rows, hd), low),
            pltpu.VMEM((blocks, blocks * BLK, BLK), f32),
            pltpu.VMEM((blocks, blocks * BLK, BLK), f32),
            pltpu.VMEM((hd, blocks * BLK), low),
            pltpu.VMEM((blocks * BLK, hd), f32),
            pltpu.VMEM((blocks * BLK, hd), f32),
            pltpu.SemaphoreType.DMA((2,)),
            pltpu.SemaphoreType.DMA((2, 4)),
        ],
        compiler_params=grant(60),
    )(temper, recv)
    back = lax.all_to_all(results, "ctx", split_axis=0, concat_axis=0, tiled=True)
    exp_size = lax.axis_size("exp")
    step = 1
    while step < exp_size:
        gt = gt + lax.ppermute(gt, "exp", [(n, (n + step) % exp_size) for n in range(exp_size)])
        step *= 2
    outs = pl.pallas_call(
        unpack_body,
        out_shape=[jax.ShapeDtypeStruct((rows, heads, hd), low)] * 4,
        in_specs=[any_spec()],
        out_specs=[any_spec()] * 4,
        scratch_shapes=[
            pltpu.VMEM((heads, 4 * rows, hd), low),
            pltpu.VMEM((4, rows // PARTS * heads, hd), f32),
            pltpu.VMEM((4, rows, heads, hd), low),
            pltpu.SemaphoreType.DMA((4 * PARTS,)),
            pltpu.SemaphoreType.DMA((4 * PARTS,)),
        ],
        compiler_params=grant(16),
    )(back)
    attn_out, grad_q, grad_k, grad_v = [part[None] for part in outs]
    return attn_out, grad_q, grad_k, grad_v, gt


def solution(mesh):
    placed = P("exp", "ctx", None, None)
    return jax.shard_map(
        body,
        mesh=mesh,
        in_specs=(placed, placed, placed, placed, P("exp", "ctx"), P()),
        out_specs=(placed, placed, placed, placed, P("ctx")),
        check_vma=False,
    )
```

```python
import functools

import jax
import jax.numpy as jnp
from jax import lax
from jax.experimental import pallas as pl
from jax.experimental.pallas import tpu as pltpu
from jax.sharding import PartitionSpec as P

NT = (((1,), (1,)), ((), ()))
NN = (((1,), (0,)), ((), ()))
TN = (((0,), (0,)), ((), ()))
LOG2E = 1.4426950408889634
HIDE = -1e30
BLK = 256
PAD = 16
PARTS = 4
MIB = 1024 * 1024


def dot(a, b, dims):
    return lax.dot_general(a, b, dims, preferred_element_type=jnp.float32)


def pack_body(q_hbm, k_hbm, v_hbm, c_hbm, hist_ref, out_hbm, held, wide, packed, in_sem, out_sem):
    _, rows, heads, hd = held.shape
    size = rows // PARTS
    loads, stores = [], []
    for stage in range(4 * PARTS):
        place, span = stage // PARTS, pl.ds(stage % PARTS * size, size)
        ref = (q_hbm, k_hbm, v_hbm, c_hbm)[place]
        load = pltpu.make_async_copy(ref.at[span], held.at[place, span], in_sem.at[stage])
        load.start()
        loads.append(load)
    ids = jnp.broadcast_to(hist_ref[...].astype(jnp.float32), (PAD, rows)).astype(jnp.bfloat16)
    for head in range(heads):
        packed[head, 4 * rows :, :] = ids
    for stage, load in enumerate(loads):
        load.wait()
        place, first, slot = stage // PARTS, stage % PARTS * size, stage % 4
        part = held[place, first : first + size]
        wide[slot] = part.astype(jnp.float32).reshape(size * heads, hd)
        for head in range(heads):
            part = wide[slot, pl.ds(head, size, stride=heads), :]
            packed[head, stage * size : (stage + 1) * size, :] = part.astype(jnp.bfloat16)
        span = pl.ds(stage * size, size if stage + 1 < len(loads) else size + PAD)
        store = pltpu.make_async_copy(
            packed.at[:, span, :], out_hbm.at[:, span, :], out_sem.at[stage]
        )
        store.start()
        stores.append(store)
    for store in stores:
        store.wait()


def unpack_body(in_hbm, a_hbm, b_hbm, c_hbm, d_hbm, held, wide, packed, in_sem, out_sem):
    _, rows, heads, hd = packed.shape
    size = rows // PARTS
    loads, stores = [], []
    for stage in range(4 * PARTS):
        span = pl.ds(stage * size, size)
        load = pltpu.make_async_copy(
            in_hbm.at[:, span, :], held.at[:, span, :], in_sem.at[stage]
        )
        load.start()
        loads.append(load)
    for stage, load in enumerate(loads):
        load.wait()
        place, span, slot = stage // PARTS, pl.ds(stage % PARTS * size, size), stage % 4
        for head in range(heads):
            part = held[head, stage * size : (stage + 1) * size, :]
            wide[slot, pl.ds(head, size, stride=heads), :] = part.astype(jnp.float32)
        packed[place, span] = wide[slot].reshape(size, heads, hd).astype(jnp.bfloat16)
        ref = (a_hbm, b_hbm, c_hbm, d_hbm)[place]
        store = pltpu.make_async_copy(packed.at[place, span], ref.at[span], out_sem.at[stage])
        store.start()
        stores.append(store)
    for store in stores:
        store.wait()


def attend_body(
    temper_ref,
    in_hbm,
    out_hbm,
    gt_ref,
    held,
    done,
    logit,
    pgrad,
    v_t,
    dk_acc,
    dv_acc,
    in_sem,
    out_sem,
):
    shards, hd = held.shape[0], held.shape[2]
    rows = done.shape[1] // 4
    per = BLK // rows
    blocks = shards // per
    group = blocks // 4
    loads = [
        pltpu.make_async_copy(in_hbm.at[n], held.at[n], in_sem.at[n]) for n in range(shards)
    ]
    for load in loads:
        load.start()
    temper = temper_ref[lax.axis_index("ctx")]
    scale = temper * hd ** (-0.5)
    logit_scale = scale * LOG2E

    def identity(size):
        return (
            lax.broadcasted_iota(jnp.int32, (size, size), 0)
            == lax.broadcasted_iota(jnp.int32, (size, size), 1)
        ).astype(jnp.bfloat16)

    eye_hd = identity(hd)
    eye_blk = identity(BLK)

    def span_of(place, low, high):
        part = held[low * per : high * per, place * rows : (place + 1) * rows, :]
        return part.reshape((high - low) * BLK, hd)

    def put(place, block, value):
        done[block * per : (block + 1) * per, place * rows : (place + 1) * rows, :] = value.astype(
            jnp.bfloat16
        ).reshape(per, rows, hd)

    def stores(block, kind):
        part = pl.ds(2 * kind * rows, 2 * rows)
        return [
            pltpu.make_async_copy(
                done.at[n, part, :], out_hbm.at[n, part, :], out_sem.at[kind, n]
            )
            for n in range(block * per, (block + 1) * per)
        ]

    def send(block, kind):
        for copy in stores(block, kind):
            copy.start()

    def turn(low, high):
        span = slice(low * BLK, high * BLK)
        v_t[:, span] = dot(eye_hd, span_of(2, low, high), NT).astype(jnp.bfloat16)

    def folded(x):
        return x.reshape(x.shape[0] // 8, 8, x.shape[1])

    edge_low, edge_high = blocks // 4, 3 * blocks // 4

    def first_key(i, edge):
        return edge if i > edge else 0

    def scores(i, edge, bound):
        low, high = first_key(i, edge), i + 1
        s = dot(span_of(1, low, high), span_of(0, i, i + 1), NT) * logit_scale
        g = dot(span_of(2, low, high), span_of(3, i, i + 1), NT)
        pgrad[i, low * BLK : high * BLK, :] = g
        cols = i * BLK + lax.broadcasted_iota(jnp.int32, (1, BLK), 1)
        lowest = jnp.where(cols >= bound, bound, 0)
        top = None
        for j in range(low, high):
            part = s[(j - low) * BLK : (j - low + 1) * BLK]
            row = lax.broadcasted_iota(jnp.int32, (BLK, BLK), 0)
            if i == edge or j == edge:
                part = jnp.where(row >= lowest - j * BLK, part, HIDE)
            if j == i:
                part = jnp.where(
                    row <= lax.broadcasted_iota(jnp.int32, (BLK, BLK), 1), part, HIDE
                )
            logit[i, j * BLK : (j + 1) * BLK, :] = part
            part = jnp.max(folded(part), axis=0)
            top = part if top is None else jnp.maximum(top, part)
        return jnp.max(top, axis=0, keepdims=True)

    def settle(i, edge, top):
        total = delta = jnp.zeros((8, BLK), jnp.float32)
        for j in range(first_key(i, edge), i + 1):
            span = slice(j * BLK, (j + 1) * BLK)
            e = jnp.exp2(logit[i, span, :] - top)
            total = total + jnp.sum(folded(e), axis=0)
            delta = delta + jnp.sum(folded(e * pgrad[i, span, :]), axis=0)
        total = jnp.sum(total, axis=0, keepdims=True)
        delta = jnp.sum(delta, axis=0, keepdims=True) / total
        return top + jnp.log2(total), delta

    def gradients(i, edge, norm, delta, gt):
        low, high = first_key(i, edge), i + 1
        weights, grads = [], []
        for j in range(low, high):
            span = slice(j * BLK, (j + 1) * BLK)
            s = logit[i, span, :]
            p = jnp.exp2(s - norm)
            ds = p * (pgrad[i, span, :] - delta)
            gt = gt + jnp.sum(folded(ds * s), axis=0)
            weights.append(p.astype(jnp.bfloat16))
            grads.append(ds.astype(jnp.bfloat16))
        p, ds = jnp.concatenate(weights, axis=0), jnp.concatenate(grads, axis=0)
        dv = dot(p, span_of(3, i, i + 1), NN)
        dk = dot(ds, span_of(0, i, i + 1), NN)
        if low < i:
            span = slice(low * BLK, i * BLK)
            dv_acc[span, :] += dv[: (i - low) * BLK]
            dk_acc[span, :] += dk[: (i - low) * BLK]
        span = slice(i * BLK, high * BLK)
        dv_acc[span, :] = dv[(i - low) * BLK :]
        dk_acc[span, :] = dk[(i - low) * BLK :]
        span = slice(low * BLK, high * BLK)
        o = dot(v_t[:, span], p, NN).astype(jnp.bfloat16)
        dq = dot(ds, span_of(1, low, high), TN) * scale
        put(0, i, dot(eye_blk, o, NT))
        put(1, i, dq)
        return gt

    def leave(first, last):
        for j in range(first, last):
            span = slice(j * BLK, (j + 1) * BLK)
            put(2, j, dk_acc[span, :] * scale)
            put(3, j, dv_acc[span, :])
            send(j, 1)

    for load in loads[: group * per]:
        load.wait()
    turn(0, group)
    everything = shards * rows
    top = scores(0, edge_high, everything)
    next_top = scores(1, edge_high, everything)
    norm, delta = settle(0, edge_high, top)
    first_gt = gradients(0, edge_high, norm, delta, jnp.zeros((8, BLK), jnp.float32))
    send(0, 0)
    for load in loads[group * per :]:
        load.wait()
    ids = held[:, 4 * rows :, :].astype(jnp.float32)
    bound = everything - (jnp.sum(ids) * (1.0 / PAD)).astype(jnp.int32)
    turn(group, blocks)
    edge_at = jnp.clip(bound // BLK, edge_low, edge_high - 1)

    def rest(edge):
        gt, top, left = first_gt, next_top, 0
        for i in range(1, blocks):
            if i + 1 < blocks:
                following = scores(i + 1, edge, bound)
            norm, delta = settle(i, edge, top)
            top = following
            gt = gradients(i, edge, norm, delta, gt)
            send(i, 0)
            if i == edge:
                left = edge
                leave(0, left)
        leave(left, blocks)
        gt_ref[0] = jnp.sum(gt) / (temper * LOG2E)

    for edge in range(edge_low, edge_high):
        pl.when(edge_at == edge)(functools.partial(rest, edge))
    for block in range(blocks):
        for kind in range(2):
            for copy in stores(block, kind):
                copy.wait()


def vmem_spec():
    return pl.BlockSpec(memory_space=pltpu.VMEM)


def any_spec():
    return pl.BlockSpec(memory_space=pl.ANY)


def grant(mib):
    return pltpu.CompilerParams(vmem_limit_bytes=mib * MIB)


def body(queries, keys, values, cotangent, history, temper):
    _, rows, heads, hd = queries.shape
    shards = lax.axis_size("ctx")
    blocks = shards * rows // BLK
    low, f32 = jnp.bfloat16, jnp.float32

    send = pl.pallas_call(
        pack_body,
        out_shape=jax.ShapeDtypeStruct((heads, 4 * rows + PAD, hd), low),
        in_specs=[any_spec()] * 4 + [vmem_spec()],
        out_specs=any_spec(),
        scratch_shapes=[
            pltpu.VMEM((4, rows, heads, hd), low),
            pltpu.VMEM((4, rows // PARTS * heads, hd), f32),
            pltpu.VMEM((heads, 4 * rows + PAD, hd), low),
            pltpu.SemaphoreType.DMA((4 * PARTS,)),
            pltpu.SemaphoreType.DMA((4 * PARTS,)),
        ],
        compiler_params=grant(56),
    )(queries[0], keys[0], values[0], cotangent[0], history)
    recv = lax.all_to_all(send, "ctx", split_axis=0, concat_axis=0, tiled=True)
    results, gt = pl.pallas_call(
        attend_body,
        out_shape=(
            jax.ShapeDtypeStruct((shards, 4 * rows, hd), low),
            jax.ShapeDtypeStruct((1,), f32),
        ),
        in_specs=[pl.BlockSpec(memory_space=pltpu.SMEM), any_spec()],
        out_specs=(any_spec(), pl.BlockSpec(memory_space=pltpu.SMEM)),
        scratch_shapes=[
            pltpu.VMEM((shards, 4 * rows + PAD, hd), low),
            pltpu.VMEM((shards, 4 * rows, hd), low),
            pltpu.VMEM((blocks, blocks * BLK, BLK), f32),
            pltpu.VMEM((blocks, blocks * BLK, BLK), f32),
            pltpu.VMEM((hd, blocks * BLK), low),
            pltpu.VMEM((blocks * BLK, hd), f32),
            pltpu.VMEM((blocks * BLK, hd), f32),
            pltpu.SemaphoreType.DMA((shards,)),
            pltpu.SemaphoreType.DMA((2, shards)),
        ],
        compiler_params=grant(60),
    )(temper, recv)
    back = lax.all_to_all(results, "ctx", split_axis=0, concat_axis=0, tiled=True)
    exp_size = lax.axis_size("exp")
    step = 1
    while step < exp_size:
        gt = gt + lax.ppermute(gt, "exp", [(n, (n + step) % exp_size) for n in range(exp_size)])
        step *= 2
    outs = pl.pallas_call(
        unpack_body,
        out_shape=[jax.ShapeDtypeStruct((rows, heads, hd), low)] * 4,
        in_specs=[any_spec()],
        out_specs=[any_spec()] * 4,
        scratch_shapes=[
            pltpu.VMEM((heads, 4 * rows, hd), low),
            pltpu.VMEM((4, rows // PARTS * heads, hd), f32),
            pltpu.VMEM((4, rows, heads, hd), low),
            pltpu.SemaphoreType.DMA((4 * PARTS,)),
            pltpu.SemaphoreType.DMA((4 * PARTS,)),
        ],
        compiler_params=grant(16),
    )(back)
    attn_out, grad_q, grad_k, grad_v = [part[None] for part in outs]
    return attn_out, grad_q, grad_k, grad_v, gt


def solution(mesh):
    placed = P("exp", "ctx", None, None)
    return jax.shard_map(
        body,
        mesh=mesh,
        in_specs=(placed, placed, placed, placed, P("exp", "ctx"), P()),
        out_specs=(placed, placed, placed, placed, P("ctx")),
        check_vma=False,
    )
```

```python
import functools

import jax
import jax.numpy as jnp
from jax import lax
from jax.experimental import pallas as pl
from jax.experimental.pallas import tpu as pltpu
from jax.sharding import PartitionSpec as P

NT = (((1,), (1,)), ((), ()))
NN = (((1,), (0,)), ((), ()))
TN = (((0,), (0,)), ((), ()))
LOG2E = 1.4426950408889634
HIDE = -1e30
BLK = 256
PAD = 16
PARTS = 2
MIB = 1024 * 1024


def dot(a, b, dims):
    return lax.dot_general(a, b, dims, preferred_element_type=jnp.float32)


def pack_body(q_hbm, k_hbm, v_hbm, c_hbm, hist_ref, out_hbm, held, wide, packed, in_sem, out_sem):
    _, rows, heads, hd = held.shape
    size = rows // PARTS
    loads, stores = [], []
    for stage in range(4 * PARTS):
        place, span = stage // PARTS, pl.ds(stage % PARTS * size, size)
        ref = (q_hbm, k_hbm, v_hbm, c_hbm)[place]
        load = pltpu.make_async_copy(ref.at[span], held.at[place, span], in_sem.at[stage])
        load.start()
        loads.append(load)
    ids = jnp.broadcast_to(hist_ref[...].astype(jnp.float32), (PAD, rows)).astype(jnp.bfloat16)
    for head in range(heads):
        packed[head, 4 * rows :, :] = ids
    for stage, load in enumerate(loads):
        load.wait()
        place, first, slot = stage // PARTS, stage % PARTS * size, stage % 4
        part = held[place, first : first + size]
        wide[slot] = part.astype(jnp.float32).reshape(size * heads, hd)
        for head in range(heads):
            part = wide[slot, pl.ds(head, size, stride=heads), :]
            packed[head, stage * size : (stage + 1) * size, :] = part.astype(jnp.bfloat16)
        span = pl.ds(stage * size, size if stage + 1 < len(loads) else size + PAD)
        store = pltpu.make_async_copy(
            packed.at[:, span, :], out_hbm.at[:, span, :], out_sem.at[stage]
        )
        store.start()
        stores.append(store)
    for store in stores:
        store.wait()


def unpack_body(held, a_hbm, b_hbm, c_hbm, d_hbm, wide, packed, out_sem):
    _, rows, heads, hd = packed.shape
    size = rows // PARTS
    stores = []
    for stage in range(4 * PARTS):
        place, span, slot = stage // PARTS, pl.ds(stage % PARTS * size, size), stage % 4
        for head in range(heads):
            part = held[head, stage * size : (stage + 1) * size, :]
            wide[slot, pl.ds(head, size, stride=heads), :] = part.astype(jnp.float32)
        packed[place, span] = wide[slot].reshape(size, heads, hd).astype(jnp.bfloat16)
        ref = (a_hbm, b_hbm, c_hbm, d_hbm)[place]
        store = pltpu.make_async_copy(packed.at[place, span], ref.at[span], out_sem.at[stage])
        store.start()
        stores.append(store)
    for store in stores:
        store.wait()


def attend_body(
    temper_ref,
    held,
    out_hbm,
    gt_ref,
    done,
    logit,
    pgrad,
    v_t,
    dk_acc,
    dv_acc,
    out_sem,
):
    shards, hd = held.shape[0], held.shape[2]
    rows = done.shape[1] // 4
    per = BLK // rows
    blocks = shards // per
    group = blocks // 4
    temper = temper_ref[lax.axis_index("ctx")]
    scale = temper * hd ** (-0.5)
    logit_scale = scale * LOG2E

    def identity(size):
        return (
            lax.broadcasted_iota(jnp.int32, (size, size), 0)
            == lax.broadcasted_iota(jnp.int32, (size, size), 1)
        ).astype(jnp.bfloat16)

    eye_hd = identity(hd)
    eye_blk = identity(BLK)

    def span_of(place, low, high):
        part = held[low * per : high * per, place * rows : (place + 1) * rows, :]
        return part.reshape((high - low) * BLK, hd)

    def put(place, block, value):
        done[block * per : (block + 1) * per, place * rows : (place + 1) * rows, :] = value.astype(
            jnp.bfloat16
        ).reshape(per, rows, hd)

    def store(first, last, kind):
        span, part = pl.ds(first * per, (last - first) * per), pl.ds(2 * kind * rows, 2 * rows)
        return pltpu.make_async_copy(
            done.at[span, part, :], out_hbm.at[span, part, :], out_sem.at[kind, first // group]
        )

    def turn(low, high):
        span = slice(low * BLK, high * BLK)
        v_t[:, span] = dot(eye_hd, span_of(2, low, high), NT).astype(jnp.bfloat16)

    def folded(x):
        return x.reshape(x.shape[0] // 8, 8, x.shape[1])

    edge_low, edge_high = blocks // 4, 3 * blocks // 4

    def first_key(i, edge):
        return edge if i > edge else 0

    def scores(i, edge, bound):
        low, high = first_key(i, edge), i + 1
        s = dot(span_of(1, low, high), span_of(0, i, i + 1), NT) * logit_scale
        g = dot(span_of(2, low, high), span_of(3, i, i + 1), NT)
        pgrad[i, low * BLK : high * BLK, :] = g
        cols = i * BLK + lax.broadcasted_iota(jnp.int32, (1, BLK), 1)
        lowest = jnp.where(cols >= bound, bound, 0)
        top = None
        for j in range(low, high):
            part = s[(j - low) * BLK : (j - low + 1) * BLK]
            row = lax.broadcasted_iota(jnp.int32, (BLK, BLK), 0)
            if i == edge or j == edge:
                part = jnp.where(row >= lowest - j * BLK, part, HIDE)
            if j == i:
                part = jnp.where(
                    row <= lax.broadcasted_iota(jnp.int32, (BLK, BLK), 1), part, HIDE
                )
            logit[i, j * BLK : (j + 1) * BLK, :] = part
            part = jnp.max(folded(part), axis=0)
            top = part if top is None else jnp.maximum(top, part)
        return jnp.max(top, axis=0, keepdims=True)

    def settle(i, edge, top):
        total = delta = jnp.zeros((8, BLK), jnp.float32)
        for j in range(first_key(i, edge), i + 1):
            span = slice(j * BLK, (j + 1) * BLK)
            e = jnp.exp2(logit[i, span, :] - top)
            total = total + jnp.sum(folded(e), axis=0)
            delta = delta + jnp.sum(folded(e * pgrad[i, span, :]), axis=0)
        total = jnp.sum(total, axis=0, keepdims=True)
        delta = jnp.sum(delta, axis=0, keepdims=True) / total
        return top + jnp.log2(total), delta

    def gradients(i, edge, norm, delta, gt):
        low, high = first_key(i, edge), i + 1
        weights, grads = [], []
        for j in range(low, high):
            span = slice(j * BLK, (j + 1) * BLK)
            s = logit[i, span, :]
            p = jnp.exp2(s - norm)
            ds = p * (pgrad[i, span, :] - delta)
            gt = gt + jnp.sum(folded(ds * s), axis=0)
            weights.append(p.astype(jnp.bfloat16))
            grads.append(ds.astype(jnp.bfloat16))
        p, ds = jnp.concatenate(weights, axis=0), jnp.concatenate(grads, axis=0)
        dv = dot(p, span_of(3, i, i + 1), NN)
        dk = dot(ds, span_of(0, i, i + 1), NN)
        if low < i:
            span = slice(low * BLK, i * BLK)
            dv_acc[span, :] += dv[: (i - low) * BLK]
            dk_acc[span, :] += dk[: (i - low) * BLK]
        span = slice(i * BLK, high * BLK)
        dv_acc[span, :] = dv[(i - low) * BLK :]
        dk_acc[span, :] = dk[(i - low) * BLK :]
        span = slice(low * BLK, high * BLK)
        o = dot(v_t[:, span], p, NN).astype(jnp.bfloat16)
        dq = dot(ds, span_of(1, low, high), TN) * scale
        put(0, i, dot(eye_blk, o, NT))
        put(1, i, dq)
        return gt

    def leave(first, last):
        for j in range(first, last):
            span = slice(j * BLK, (j + 1) * BLK)
            put(2, j, dk_acc[span, :] * scale)
            put(3, j, dv_acc[span, :])
            if (j + 1) % group == 0:
                store(j + 1 - group, j + 1, 1).start()

    turn(0, group)
    everything = shards * rows
    top = scores(0, edge_high, everything)
    next_top = scores(1, edge_high, everything)
    norm, delta = settle(0, edge_high, top)
    first_gt = gradients(0, edge_high, norm, delta, jnp.zeros((8, BLK), jnp.float32))
    ids = held[:, 4 * rows :, :].astype(jnp.float32)
    bound = everything - (jnp.sum(ids) * (1.0 / PAD)).astype(jnp.int32)
    turn(group, blocks)
    edge_at = jnp.clip(bound // BLK, edge_low, edge_high - 1)

    def rest(edge):
        gt, top, left = first_gt, next_top, 0
        for i in range(1, blocks):
            if i + 1 < blocks:
                following = scores(i + 1, edge, bound)
            norm, delta = settle(i, edge, top)
            top = following
            gt = gradients(i, edge, norm, delta, gt)
            if (i + 1) % group == 0:
                store(i + 1 - group, i + 1, 0).start()
            if i == edge:
                left = edge // group * group
                leave(0, left)
        leave(left, blocks)
        gt_ref[0] = jnp.sum(gt) / (temper * LOG2E)

    for edge in range(edge_low, edge_high):
        pl.when(edge_at == edge)(functools.partial(rest, edge))
    for first in range(0, blocks, group):
        store(first, first + group, 0).wait()
        store(first, first + group, 1).wait()


def vmem_spec():
    return pl.BlockSpec(memory_space=pltpu.VMEM)


def any_spec():
    return pl.BlockSpec(memory_space=pl.ANY)


def grant(mib):
    return pltpu.CompilerParams(vmem_limit_bytes=mib * MIB)


def body(queries, keys, values, cotangent, history, temper):
    _, rows, heads, hd = queries.shape
    shards = lax.axis_size("ctx")
    blocks = shards * rows // BLK
    low, f32 = jnp.bfloat16, jnp.float32

    send = pl.pallas_call(
        pack_body,
        out_shape=jax.ShapeDtypeStruct((heads, 4 * rows + PAD, hd), low),
        in_specs=[any_spec()] * 4 + [vmem_spec()],
        out_specs=any_spec(),
        scratch_shapes=[
            pltpu.VMEM((4, rows, heads, hd), low),
            pltpu.VMEM((4, rows // PARTS * heads, hd), f32),
            pltpu.VMEM((heads, 4 * rows + PAD, hd), low),
            pltpu.SemaphoreType.DMA((4 * PARTS,)),
            pltpu.SemaphoreType.DMA((4 * PARTS,)),
        ],
        compiler_params=grant(56),
    )(queries[0], keys[0], values[0], cotangent[0], history)
    recv = lax.all_to_all(send, "ctx", split_axis=0, concat_axis=0, tiled=True)
    results, gt = pl.pallas_call(
        attend_body,
        out_shape=(
            jax.ShapeDtypeStruct((shards, 4 * rows, hd), low),
            jax.ShapeDtypeStruct((1,), f32),
        ),
        in_specs=[pl.BlockSpec(memory_space=pltpu.SMEM), vmem_spec()],
        out_specs=(any_spec(), pl.BlockSpec(memory_space=pltpu.SMEM)),
        scratch_shapes=[
            pltpu.VMEM((shards, 4 * rows, hd), low),
            pltpu.VMEM((blocks, blocks * BLK, BLK), f32),
            pltpu.VMEM((blocks, blocks * BLK, BLK), f32),
            pltpu.VMEM((hd, blocks * BLK), low),
            pltpu.VMEM((blocks * BLK, hd), f32),
            pltpu.VMEM((blocks * BLK, hd), f32),
            pltpu.SemaphoreType.DMA((2, 4)),
        ],
        compiler_params=grant(50),
    )(temper, pltpu.with_memory_space_constraint(recv, pltpu.VMEM))
    back = lax.all_to_all(results, "ctx", split_axis=0, concat_axis=0, tiled=True)
    exp_size = lax.axis_size("exp")
    step = 1
    while step < exp_size:
        gt = gt + lax.ppermute(gt, "exp", [(n, (n + step) % exp_size) for n in range(exp_size)])
        step *= 2
    outs = pl.pallas_call(
        unpack_body,
        out_shape=[jax.ShapeDtypeStruct((rows, heads, hd), low)] * 4,
        in_specs=[vmem_spec()],
        out_specs=[any_spec()] * 4,
        scratch_shapes=[
            pltpu.VMEM((4, rows // PARTS * heads, hd), f32),
            pltpu.VMEM((4, rows, heads, hd), low),
            pltpu.SemaphoreType.DMA((4 * PARTS,)),
        ],
        compiler_params=grant(16),
    )(pltpu.with_memory_space_constraint(back, pltpu.VMEM))
    attn_out, grad_q, grad_k, grad_v = [part[None] for part in outs]
    return attn_out, grad_q, grad_k, grad_v, gt


def solution(mesh):
    placed = P("exp", "ctx", None, None)
    return jax.shard_map(
        body,
        mesh=mesh,
        in_specs=(placed, placed, placed, placed, P("exp", "ctx"), P()),
        out_specs=(placed, placed, placed, placed, P("ctx")),
        check_vma=False,
    )
```

```python
import functools

import jax
import jax.numpy as jnp
from jax import lax
from jax.experimental import pallas as pl
from jax.experimental.pallas import tpu as pltpu
from jax.sharding import PartitionSpec as P

NT = (((1,), (1,)), ((), ()))
NN = (((1,), (0,)), ((), ()))
TN = (((0,), (0,)), ((), ()))
LOG2E = 1.4426950408889634
HIDE = -1e30
BLK = 256
PAD = 16
PARTS = 2
MIB = 1024 * 1024


def dot(a, b, dims):
    return lax.dot_general(a, b, dims, preferred_element_type=jnp.float32)


def pack_body(q_hbm, k_hbm, v_hbm, c_hbm, hist_ref, out_hbm, held, wide, packed, in_sem, out_sem):
    _, rows, heads, hd = held.shape
    size = rows // PARTS
    loads, stores = [], []
    for stage in range(4 * PARTS):
        place, span = stage // PARTS, pl.ds(stage % PARTS * size, size)
        ref = (q_hbm, k_hbm, v_hbm, c_hbm)[place]
        load = pltpu.make_async_copy(ref.at[span], held.at[place, span], in_sem.at[stage])
        load.start()
        loads.append(load)
    ids = jnp.broadcast_to(hist_ref[...].astype(jnp.float32), (PAD, rows)).astype(jnp.bfloat16)
    for head in range(heads):
        packed[head, 4 * rows :, :] = ids
    for stage, load in enumerate(loads):
        load.wait()
        place, first, slot = stage // PARTS, stage % PARTS * size, stage % 4
        part = held[place, first : first + size]
        wide[slot] = part.astype(jnp.float32).reshape(size * heads, hd)
        for head in range(heads):
            part = wide[slot, pl.ds(head, size, stride=heads), :]
            packed[head, stage * size : (stage + 1) * size, :] = part.astype(jnp.bfloat16)
        span = pl.ds(stage * size, size if stage + 1 < len(loads) else size + PAD)
        store = pltpu.make_async_copy(
            packed.at[:, span, :], out_hbm.at[:, span, :], out_sem.at[stage]
        )
        store.start()
        stores.append(store)
    for store in stores:
        store.wait()


def unpack_body(held, a_hbm, b_hbm, c_hbm, d_hbm, wide, packed, out_sem):
    _, rows, heads, hd = packed.shape
    size = rows // PARTS
    stores = []
    for stage in range(4 * PARTS):
        place, span, slot = stage // PARTS, pl.ds(stage % PARTS * size, size), stage % 4
        for head in range(heads):
            part = held[head, stage * size : (stage + 1) * size, :]
            wide[slot, pl.ds(head, size, stride=heads), :] = part.astype(jnp.float32)
        packed[place, span] = wide[slot].reshape(size, heads, hd).astype(jnp.bfloat16)
        ref = (a_hbm, b_hbm, c_hbm, d_hbm)[place]
        store = pltpu.make_async_copy(packed.at[place, span], ref.at[span], out_sem.at[stage])
        store.start()
        stores.append(store)
    for store in stores:
        store.wait()


def attend_body(
    temper_ref,
    held,
    out_hbm,
    gt_ref,
    done,
    logit,
    pgrad,
    v_t,
    dk_acc,
    dv_acc,
    out_sem,
):
    shards, hd = held.shape[0], held.shape[2]
    rows = done.shape[1] // 4
    per = BLK // rows
    blocks = shards // per
    group = blocks // 4
    temper = temper_ref[lax.axis_index("ctx")]
    scale = temper * hd ** (-0.5)
    logit_scale = scale * LOG2E

    def identity(size):
        return (
            lax.broadcasted_iota(jnp.int32, (size, size), 0)
            == lax.broadcasted_iota(jnp.int32, (size, size), 1)
        ).astype(jnp.bfloat16)

    eye_hd = identity(hd)
    eye_blk = identity(BLK)

    def span_of(place, low, high):
        part = held[low * per : high * per, place * rows : (place + 1) * rows, :]
        return part.reshape((high - low) * BLK, hd)

    def put(place, block, value):
        done[block * per : (block + 1) * per, place * rows : (place + 1) * rows, :] = value.astype(
            jnp.bfloat16
        ).reshape(per, rows, hd)

    def store(first, last, kind):
        span, part = pl.ds(first * per, (last - first) * per), pl.ds(2 * kind * rows, 2 * rows)
        return pltpu.make_async_copy(
            done.at[span, part, :], out_hbm.at[span, part, :], out_sem.at[kind, first]
        )

    def turn(low, high):
        span = slice(low * BLK, high * BLK)
        v_t[:, span] = dot(eye_hd, span_of(2, low, high), NT).astype(jnp.bfloat16)

    def folded(x):
        return x.reshape(x.shape[0] // 8, 8, x.shape[1])

    edge_low, edge_high = blocks // 4, 3 * blocks // 4

    def first_key(i, edge):
        return edge if i > edge else 0

    def scores(i, edge, bound):
        low, high = first_key(i, edge), i + 1
        s = dot(span_of(1, low, high), span_of(0, i, i + 1), NT) * logit_scale
        g = dot(span_of(2, low, high), span_of(3, i, i + 1), NT)
        pgrad[i, low * BLK : high * BLK, :] = g
        cols = i * BLK + lax.broadcasted_iota(jnp.int32, (1, BLK), 1)
        lowest = jnp.where(cols >= bound, bound, 0)
        top = None
        for j in range(low, high):
            part = s[(j - low) * BLK : (j - low + 1) * BLK]
            row = lax.broadcasted_iota(jnp.int32, (BLK, BLK), 0)
            if i == edge or j == edge:
                part = jnp.where(row >= lowest - j * BLK, part, HIDE)
            if j == i:
                part = jnp.where(
                    row <= lax.broadcasted_iota(jnp.int32, (BLK, BLK), 1), part, HIDE
                )
            logit[i, j * BLK : (j + 1) * BLK, :] = part
            part = jnp.max(folded(part), axis=0)
            top = part if top is None else jnp.maximum(top, part)
        return jnp.max(top, axis=0, keepdims=True)

    def settle(i, edge, top):
        total = delta = jnp.zeros((8, BLK), jnp.float32)
        for j in range(first_key(i, edge), i + 1):
            span = slice(j * BLK, (j + 1) * BLK)
            e = jnp.exp2(logit[i, span, :] - top)
            total = total + jnp.sum(folded(e), axis=0)
            delta = delta + jnp.sum(folded(e * pgrad[i, span, :]), axis=0)
        total = jnp.sum(total, axis=0, keepdims=True)
        delta = jnp.sum(delta, axis=0, keepdims=True) / total
        return top + jnp.log2(total), delta

    def gradients(i, edge, norm, delta, gt):
        low, high = first_key(i, edge), i + 1
        weights, grads = [], []
        for j in range(low, high):
            span = slice(j * BLK, (j + 1) * BLK)
            s = logit[i, span, :]
            p = jnp.exp2(s - norm)
            ds = p * (pgrad[i, span, :] - delta)
            gt = gt + jnp.sum(folded(ds * s), axis=0)
            weights.append(p.astype(jnp.bfloat16))
            grads.append(ds.astype(jnp.bfloat16))
        p, ds = jnp.concatenate(weights, axis=0), jnp.concatenate(grads, axis=0)
        dv = dot(p, span_of(3, i, i + 1), NN)
        dk = dot(ds, span_of(0, i, i + 1), NN)
        if low < i:
            span = slice(low * BLK, i * BLK)
            dv_acc[span, :] += dv[: (i - low) * BLK]
            dk_acc[span, :] += dk[: (i - low) * BLK]
        span = slice(i * BLK, high * BLK)
        dv_acc[span, :] = dv[(i - low) * BLK :]
        dk_acc[span, :] = dk[(i - low) * BLK :]
        span = slice(low * BLK, high * BLK)
        o = dot(v_t[:, span], p, NN).astype(jnp.bfloat16)
        dq = dot(ds, span_of(1, low, high), TN) * scale
        put(0, i, dot(eye_blk, o, NT))
        put(1, i, dq)
        return gt

    def leave(first, last):
        for j in range(first, last):
            span = slice(j * BLK, (j + 1) * BLK)
            put(2, j, dk_acc[span, :] * scale)
            put(3, j, dv_acc[span, :])
            store(j, j + 1, 1).start()

    everything = shards * rows
    ids = held[:, 4 * rows :, :].astype(jnp.float32)
    bound = everything - (jnp.sum(ids) * (1.0 / PAD)).astype(jnp.int32)
    turn(0, group)
    top = scores(0, edge_high, everything)
    next_top = scores(1, edge_high, everything)
    norm, delta = settle(0, edge_high, top)
    first_gt = gradients(0, edge_high, norm, delta, jnp.zeros((8, BLK), jnp.float32))
    store(0, 1, 0).start()
    turn(group, blocks)
    edge_at = jnp.clip(bound // BLK, edge_low, edge_high - 1)

    def rest(edge):
        gt, top, left = first_gt, next_top, 0
        for i in range(1, blocks):
            if i + 1 < blocks:
                following = scores(i + 1, edge, bound)
            norm, delta = settle(i, edge, top)
            top = following
            gt = gradients(i, edge, norm, delta, gt)
            store(i, i + 1, 0).start()
            if i == edge:
                left = edge
                leave(0, left)
        leave(left, blocks)
        gt_ref[0] = jnp.sum(gt) / (temper * LOG2E)

    for edge in range(edge_low, edge_high):
        pl.when(edge_at == edge)(functools.partial(rest, edge))
    for block in range(blocks):
        store(block, block + 1, 0).wait()
        store(block, block + 1, 1).wait()


def vmem_spec():
    return pl.BlockSpec(memory_space=pltpu.VMEM)


def any_spec():
    return pl.BlockSpec(memory_space=pl.ANY)


def grant(mib):
    return pltpu.CompilerParams(vmem_limit_bytes=mib * MIB)


def body(queries, keys, values, cotangent, history, temper):
    _, rows, heads, hd = queries.shape
    shards = lax.axis_size("ctx")
    blocks = shards * rows // BLK
    low, f32 = jnp.bfloat16, jnp.float32

    send = pl.pallas_call(
        pack_body,
        out_shape=jax.ShapeDtypeStruct((heads, 4 * rows + PAD, hd), low),
        in_specs=[any_spec()] * 4 + [vmem_spec()],
        out_specs=any_spec(),
        scratch_shapes=[
            pltpu.VMEM((4, rows, heads, hd), low),
            pltpu.VMEM((4, rows // PARTS * heads, hd), f32),
            pltpu.VMEM((heads, 4 * rows + PAD, hd), low),
            pltpu.SemaphoreType.DMA((4 * PARTS,)),
            pltpu.SemaphoreType.DMA((4 * PARTS,)),
        ],
        compiler_params=grant(56),
    )(queries[0], keys[0], values[0], cotangent[0], history)
    recv = lax.all_to_all(send, "ctx", split_axis=0, concat_axis=0, tiled=True)
    results, gt = pl.pallas_call(
        attend_body,
        out_shape=(
            jax.ShapeDtypeStruct((shards, 4 * rows, hd), low),
            jax.ShapeDtypeStruct((1,), f32),
        ),
        in_specs=[pl.BlockSpec(memory_space=pltpu.SMEM), vmem_spec()],
        out_specs=(any_spec(), pl.BlockSpec(memory_space=pltpu.SMEM)),
        scratch_shapes=[
            pltpu.VMEM((shards, 4 * rows, hd), low),
            pltpu.VMEM((blocks, blocks * BLK, BLK), f32),
            pltpu.VMEM((blocks, blocks * BLK, BLK), f32),
            pltpu.VMEM((hd, blocks * BLK), low),
            pltpu.VMEM((blocks * BLK, hd), f32),
            pltpu.VMEM((blocks * BLK, hd), f32),
            pltpu.SemaphoreType.DMA((2, blocks)),
        ],
        compiler_params=grant(50),
    )(temper, pltpu.with_memory_space_constraint(recv, pltpu.VMEM))
    back = lax.all_to_all(results, "ctx", split_axis=0, concat_axis=0, tiled=True)
    exp_size = lax.axis_size("exp")
    step = 1
    while step < exp_size:
        gt = gt + lax.ppermute(gt, "exp", [(n, (n + step) % exp_size) for n in range(exp_size)])
        step *= 2
    outs = pl.pallas_call(
        unpack_body,
        out_shape=[jax.ShapeDtypeStruct((rows, heads, hd), low)] * 4,
        in_specs=[vmem_spec()],
        out_specs=[any_spec()] * 4,
        scratch_shapes=[
            pltpu.VMEM((4, rows // PARTS * heads, hd), f32),
            pltpu.VMEM((4, rows, heads, hd), low),
            pltpu.SemaphoreType.DMA((4 * PARTS,)),
        ],
        compiler_params=grant(16),
    )(pltpu.with_memory_space_constraint(back, pltpu.VMEM))
    attn_out, grad_q, grad_k, grad_v = [part[None] for part in outs]
    return attn_out, grad_q, grad_k, grad_v, gt


def solution(mesh):
    placed = P("exp", "ctx", None, None)
    return jax.shard_map(
        body,
        mesh=mesh,
        in_specs=(placed, placed, placed, placed, P("exp", "ctx"), P()),
        out_specs=(placed, placed, placed, placed, P("ctx")),
        check_vma=False,
    )
```
